128 devices in a mesh: replica: 8 (over z, y_lo), tensor: 16 (over x, y_hi, core).
Axes of the slice: x: 4, y: 4 (y_hi: 2, y_lo: 2; y = y_hi * 2 + y_lo), z: 4, core: 2. Of those that a mesh axis runs over, the one named last changes fastest.
Arguments:
- hidden_in: bfloat16 [2, 128, 8192], P(None, 'replica'), may hold values from -6 to 6
- norm_gain: float32 [8192], replicated, may hold values from 0.1 to 1.9
- qkv_buckets: bfloat16 [256, 32, 10240], P(('replica', 'tensor')), may hold values from -0.0625 to 0.0625
- bucket_slot: int32 [256], replicated, may hold values from 0 to 255, each once
- kv_cache: bfloat16 [128, 16384, 256], P('replica', 'tensor')
- cache_len: int32 [128], P('replica'), may hold values from 1 to 2048, as said below
Outputs:
- context: bfloat16 [2, 128, 8192], P(None, 'replica', 'tensor')
- served_weight: bfloat16 [16, 8192, 768], P('tensor')
The draws below stay inside these ranges and needn't reach their ends.
Inputs may be any that keep to these rules, and one draw needn't show every extreme that they name: `cache_len`: each row has at least one valid cached position, and some row holds all 2048.
All inputs are finite; a program needn't handle non-finite values.
Results may differ from the reference program's by a relative error of at most 0.015.
The reference program's roundings to bfloat16 on the way (of `weight`, `normed` and `probs`) count: a program that leaves them out, or rounds other values in their place, can miss the bound.
Values may be sent and summed in bfloat16 or wider, within the bound.
A program may use at most 128 MiB of HBM per device.

```python
import jax
import jax.numpy as jnp
from jax import lax

D = 8192
QH = 64
KVH = 8
HD = 128
LEN = 2048
STEPS = 2
BROWS = 32
QD = 8192
KVD = 1024
NBUCKETS = 256
ROWS_ALL = 128
N_TENSOR = 16


def draw_kv_cache(key, part):
    key = jax.random.fold_in(key, 11)
    first_key = jax.random.fold_in(key, 0)
    values = jax.random.normal(first_key, (ROWS_ALL, KVH * LEN, 2 * HD), jnp.float32)
    return values.astype(jnp.bfloat16)


def draw_cache_len(key, part):
    key = jax.random.fold_in(key, 5)
    first_key, second_key = jax.random.split(key, 2)
    lengths = jax.random.randint(first_key, (ROWS_ALL,), 1, LEN + 1)
    chosen = jax.random.randint(second_key, (), 0, ROWS_ALL)
    return jnp.where(jnp.arange(ROWS_ALL) == chosen, LEN, lengths).astype(jnp.int32)


def block_scale(rng, dims, shards, low, high):
    level, own = 1.0, jax.random.fold_in(rng, 6)
    for position, shards_of in shards:
        draws = jnp.exp(jax.random.uniform(jax.random.fold_in(own, position), (shards_of,), jnp.float32, low / len(shards), high / len(shards)))
        level = level * jnp.repeat(draws, dims[position] // shards_of).reshape([-1 if axis == position else 1 for axis in range(len(dims))])
    return level


def scatter_about(own_key, extent, scale, bound, cuts=(), kind=jnp.bfloat16):
    level = block_scale(own_key, extent, cuts, -0.22, 0.18) if cuts else 1.0
    result = jax.random.normal(own_key, extent, jnp.float32) * scale * level
    return jnp.minimum(jnp.maximum(result, -bound), bound).astype(kind)


def setup_inputs(seed: int = 0) -> dict:
    splits = jax.random.split(jax.random.key(seed), 7)
    return {
        "hidden_in": scatter_about(splits[0], (STEPS, ROWS_ALL, D), 1.0, 6.0, ((1, 8),)),
        "norm_gain": jnp.clip(1.0 + 0.18 * jax.random.normal(splits[1], (D,), jnp.float32), 0.1, 1.9),
        "qkv_buckets": scatter_about(splits[2], (NBUCKETS, BROWS, QD + 2 * KVD), D ** -0.5, 0.0625, ((0, 128),)),
        "bucket_slot": jax.random.permutation(splits[3], NBUCKETS).astype(jnp.int32),
        "kv_cache": draw_kv_cache(jax.random.fold_in(splits[6], 71), 0),
        "cache_len": draw_cache_len(jax.random.fold_in(splits[6], 71), 0),
    }


rope_base = 500000.0
norm_eps = 1e-05

def rotate(vectors, positions):
    half_dim = HD // 2
    freqs = rope_base ** (-2.0 * jnp.arange(half_dim, dtype=jnp.float32) / HD)
    angles = positions.astype(jnp.float32)[..., None] * freqs
    cosine = jnp.cos(angles)
    sine = jnp.sin(angles)
    first = vectors[..., :half_dim]
    second = vectors[..., half_dim:]
    return jnp.concatenate([first * cosine - second * sine, second * cosine + first * sine], axis=-1)

def attend_row(queries, keys_new, values_new, cache_row, length):
    scale_factor = HD ** (-0.5)
    cache_keys = cache_row[..., :HD].astype(jnp.float32)
    cache_values = cache_row[..., HD:].astype(jnp.float32)
    query_f = queries.astype(jnp.float32)
    scores = jnp.einsum('shgd,hpd->shgp', query_f, cache_keys) * scale_factor
    valid = jnp.arange(LEN) < length
    scores = jnp.where(valid, scores, -jnp.inf)
    fresh = jnp.einsum('shgd,thd->shgt', query_f, keys_new.astype(jnp.float32)) * scale_factor
    causal = jnp.arange(STEPS)[None, :] <= jnp.arange(STEPS)[:, None]
    fresh = jnp.where(causal[:, None, None, :], fresh, -jnp.inf)
    peaks = jnp.maximum(lax.optimization_barrier(jnp.max(scores, axis=-1)), lax.optimization_barrier(jnp.max(fresh, axis=-1)))
    probs = lax.optimization_barrier(jnp.exp(scores - peaks[..., None]).astype(jnp.bfloat16)).astype(jnp.float32)
    probs_new = lax.optimization_barrier(jnp.exp(fresh - peaks[..., None]).astype(jnp.bfloat16)).astype(jnp.float32)
    numer = jnp.einsum('shgp,hpd->shgd', probs, cache_values)
    numer = numer + jnp.einsum('shgt,thd->shgd', probs_new, values_new.astype(jnp.float32))
    denom = lax.optimization_barrier(jnp.sum(probs, axis=-1)) + lax.optimization_barrier(jnp.sum(probs_new, axis=-1))
    return (numer / denom[..., None]).astype(jnp.bfloat16)

def reference(hidden_in, norm_gain, qkv_buckets, bucket_slot, kv_cache, cache_len):
    weight = qkv_buckets[bucket_slot].reshape(D, QD + 2 * KVD)
    group_count = N_TENSOR // KVH
    query_cols = weight[:, :QD].reshape(D, N_TENSOR, QD // N_TENSOR)
    key_cols = jnp.repeat(weight[:, QD:QD + KVD].reshape(D, KVH, HD), group_count, axis=1)
    value_cols = jnp.repeat(weight[:, QD + KVD:].reshape(D, KVH, HD), group_count, axis=1)
    served_weight = jnp.transpose(jnp.concatenate([query_cols, key_cols, value_cols], axis=2), (1, 0, 2))
    inputs = hidden_in.astype(jnp.float32)
    normed = inputs * lax.rsqrt(lax.optimization_barrier(jnp.mean(inputs * inputs, axis=-1, keepdims=True)) + norm_eps) * norm_gain
    normed = normed.astype(jnp.bfloat16)
    projected = jnp.dot(normed.reshape(STEPS * ROWS_ALL, D), weight, preferred_element_type=jnp.float32)
    projected = projected.reshape(STEPS, ROWS_ALL, QD + 2 * KVD)
    positions = cache_len[None, :] + jnp.arange(STEPS, dtype=jnp.int32)[:, None]
    queries = rotate(projected[..., :QD].reshape(STEPS, ROWS_ALL, QH, HD), positions[..., None]).astype(jnp.bfloat16)
    keys_new = rotate(projected[..., QD:QD + KVD].reshape(STEPS, ROWS_ALL, KVH, HD), positions[..., None]).astype(jnp.bfloat16)
    values_new = projected[..., QD + KVD:].reshape(STEPS, ROWS_ALL, KVH, HD).astype(jnp.bfloat16)
    cache_all = kv_cache.reshape(ROWS_ALL, KVH, LEN, 2 * HD)
    group_size = QH // KVH
    grouped = queries.reshape(STEPS, ROWS_ALL, KVH, group_size, HD)

    def one_row(row_index):
        return attend_row(grouped[:, row_index], keys_new[:, row_index], values_new[:, row_index], cache_all[row_index], cache_len[row_index])
    outputs = lax.map(one_row, jnp.arange(ROWS_ALL, dtype=jnp.int32))
    context = jnp.transpose(outputs, (1, 0, 2, 3, 4)).reshape(STEPS, ROWS_ALL, QD)
    return (context, served_weight)
```

```python
import functools
import heapq
import itertools

import jax
import jax.numpy as jnp
import numpy as np
from jax import lax
from jax.experimental import pallas as pl
from jax.experimental.pallas import tpu as pltpu
from jax.sharding import PartitionSpec as P

QH = 64
KVH = 8
HD = 128
D = 8192
LEN = 2048
STEPS = 2
BROWS = 32
NB = 256
N_TENSOR = 16
N_REPLICA = 8
ROWS = 16
M = STEPS * ROWS
QC = 512
OWN = QC + HD
COLS = QC + 2 * HD
HEADS = QC // HD
HALF = LEN // 2

rope_base = 500000.0
norm_eps = 1e-05
masked_score = -1e30

MESH = pl.DeviceIdType.MESH

UNITS = ((0, 0), (1, 0), (3, 0), (0, 1), (1, 1), (3, 1), (2, 0), (2, 1))
ITEMS = ((0, 0, 2), (0, 2, 2)) + tuple((u, 0, 4) for u in range(1, 8))
PAIR_FIRST = frozenset((0, 2, 4, 5, 7))


def event_order():
    per_slot, hop = 0.87, 0.8
    entry = (0.8, 1.2, 4.0, 4.0, 4.5, 7.5, 8.5, 13.0, 14.0)
    links = ("pair", "up", "down")
    free = dict.fromkeys(links, 0.0)
    queue = {link: [] for link in links}
    count = itertools.count()
    events = [(entry[i], next(count), ("entry", i)) for i in range(len(ITEMS))]
    heapq.heapify(events)
    order = []
    while events:
        now, _, event = heapq.heappop(events)
        if event is not None:
            order.append(event)
            for link, arrival, slots in forwards(event):
                queue[link].append((arrival, slots))
        for link in links:
            if queue[link] and free[link] <= now + 1e-9:
                arrival, slots = queue[link].pop(0)
                free[link] = now + slots * per_slot
                heapq.heappush(events, (free[link] + hop, next(count), arrival))
                heapq.heappush(events, (free[link], next(count), None))
    return order


def forwards(event):
    kind, item = event[0], event[1]
    slots = ITEMS[item][2]
    sends = []
    if kind == "entry":
        sends += [("pair", ("pair", item), slots)]
        sends += [("up", ("up1", item, 0), slots), ("down", ("down1", item, 0), slots)]
    elif kind == "pair" and item in PAIR_FIRST:
        sends += [("up", ("up1", item, 1), slots), ("down", ("down1", item, 1), slots)]
    elif kind in ("up1", "down1"):
        link = kind[:-1]
        sends += [(link, (link + "2", item, event[2]), slots // 2)]
        if item not in PAIR_FIRST:
            sends += [("pair", ("late", item, kind), slots)]
    elif kind in ("up2", "down2") and item not in PAIR_FIRST:
        sends += [("pair", ("late", item, kind), slots // 2)]
    return sends


EVENTS = event_order()
PLACE = {event: i for i, event in enumerate(EVENTS)}


def gather_kernel(
    hid_hbm,
    gain_hbm,
    buckets,
    slot_hbm,
    cache,
    freq_ref,
    len_ref,
    arr,
    proj,
    cos_ref,
    sin_ref,
    cache_other,
    hid,
    gain,
    slot_row,
    inv_row,
    inv,
    turned,
    lhs,
    local_sem,
    prep_sem,
    own_sem,
    recv_sem,
    entry_sem,
    link_sem,
    stage_sem,
    kv_send,
    kv_recv,
    cache_send,
    cache_recv,
):
    r = lax.axis_index("replica")
    t = lax.axis_index("tensor")
    z, p = r // 2, r % 2
    x, h, c = t // 4, (t // 2) % 2, t % 2
    other_core = (r, x * 4 + h * 2 + (1 - c))
    target = {
        "pair": (z * 2 + (1 - p), t),
        "up": (((z + 1) % 4) * 2 + p, t),
        "down": (((z + 3) % 4) * 2 + p, t),
    }
    own_col = pl.multiple_of(QC + HD * c, HD)
    other_col = pl.multiple_of(QC + HD * (1 - c), HD)

    prep = [
        pltpu.make_async_copy(hid_hbm, hid, prep_sem.at[0]),
        pltpu.make_async_copy(gain_hbm, gain, prep_sem.at[1]),
        pltpu.make_async_copy(slot_hbm, slot_row, prep_sem.at[2]),
    ]
    for copy in prep:
        copy.start()

    def chip(dx, dh, core):
        return (z * 2 + (p + dh) % 2, ((x + dx) % 4) * 4 + ((h + dh) % 2) * 2 + core)

    barrier = pltpu.get_barrier_semaphore()
    peers = [other_core] + list(target.values())
    peers += [chip(dx, dh, core) for dx, dh in UNITS[1:] for core in range(2)]
    for peer in peers:
        pl.semaphore_signal(barrier, inc=1, device_id=peer, device_id_type=MESH)
    pl.semaphore_wait(barrier, len(peers))

    mine = (r * N_TENSOR + t) * 2

    def parts(base, slots):
        rows = pl.ds(base, slots)
        return arr.at[rows, :, pl.ds(0, QC)], arr.at[rows, :, pl.ds(own_col, HD)]

    def bucket_parts(x_to, h_to, core):
        group = x_to * 2 + h_to
        query = pl.multiple_of((group * 2 + core) * QC, QC)
        key = pl.multiple_of(QH * HD + core * (KVH * HD) + group * HD, HD)
        return buckets.at[:, :, pl.ds(query, QC)], buckets.at[:, :, pl.ds(key, HD)]

    def send_unit(unit):
        dx, dh = UNITS[unit]
        x_to, h_to, p_to = (x + 4 - dx) % 4, (h + dh) % 2, (p + dh) % 2
        for core in range(2):
            dst = (z * 2 + p_to, x_to * 4 + h_to * 2 + core)
            source = bucket_parts(x_to, h_to, core)
            cols = (pl.ds(0, QC), pl.ds(QC + HD * core, HD))
            for src, col in zip(source, cols):
                pltpu.make_async_remote_copy(
                    src_ref=src,
                    dst_ref=arr.at[pl.ds(mine, 2), :, col],
                    send_sem=stage_sem.at[0],
                    recv_sem=entry_sem.at[2 * unit + c],
                    device_id=dst,
                    device_id_type=MESH,
                ).start()

    def wait_bytes(slots, sem):
        ref = arr.at[pl.ds(0, slots), :, pl.ds(0, OWN)]
        pltpu.make_async_copy(ref, ref, sem).wait()

    own_copies = []
    for src, dst in zip(bucket_parts(x, h, c), parts(mine, 2)):
        copy = pltpu.make_async_copy(src, dst, own_sem.at[len(own_copies)])
        copy.start()
        own_copies.append(copy)
    for src, col in zip(bucket_parts(x, h, 1 - c), (pl.ds(0, QC), pl.ds(other_col, HD))):
        pltpu.make_async_remote_copy(
            src_ref=src,
            dst_ref=arr.at[pl.ds(mine, 2), :, col],
            send_sem=stage_sem.at[0],
            recv_sem=entry_sem.at[0],
            device_id=other_core,
            device_id_type=MESH,
        ).start()
    for unit in (1, 2, 3):
        send_unit(unit)

    def unit_base(unit, z_of, p_of):
        dx, dh = UNITS[unit]
        source = z_of * 2 + (p_of + dh) % 2
        return source * 32 + ((x + dx) % 4) * 8 + ((h + dh) % 2) * 4

    up_z, down_z, far_z = (z + 3) % 4, (z + 1) % 4, (z + 2) % 4

    def place(event):
        kind, item = event[0], event[1]
        unit, first, slots = ITEMS[item]
        if kind == "entry":
            z_of, p_of = z, p
        elif kind == "pair":
            z_of, p_of = z, 1 - p
        else:
            way = event[2] if kind == "late" else kind
            z_of = {"up1": up_z, "down1": down_z, "up2": far_z, "down2": far_z}[way]
            if kind == "late":
                p_of = 1 - p
            else:
                p_of = (p + event[2]) % 2
            if way in ("up2", "down2"):
                slots = slots // 2
                if way == "down2":
                    first = first + slots
        base = unit_base(unit, z_of, p_of)
        if unit == 0:
            own_half = 2 * c if item == 0 else 2 * (1 - c)
            base = base + own_half + (first - ITEMS[item][1])
        else:
            base = base + first
        return base, slots

    def wait_for(event):
        if event == ("entry", 0):
            for copy in own_copies:
                copy.wait()
        elif event == ("entry", 1):
            wait_bytes(2, entry_sem.at[0])
        elif event[0] == "entry":
            unit = ITEMS[event[1]][0]
            for core in range(2):
                wait_bytes(2, entry_sem.at[2 * unit + core])
        else:
            wait_bytes(place(event)[1], recv_sem.at[PLACE[event]])

    sent = {"pair": 0, "up": 0, "down": 0}
    link_index = {"pair": 0, "up": 1, "down": 2}

    def forward(event):
        base, _ = place(event)
        for link, arrival, slots in forwards(event):
            start = base
            if arrival[0] == "down2":
                start = base + slots
            for ref in parts(start, slots):
                pltpu.make_async_remote_copy(
                    src_ref=ref,
                    dst_ref=ref,
                    send_sem=link_sem.at[link_index[link]],
                    recv_sem=recv_sem.at[PLACE[arrival]],
                    device_id=target[link],
                    device_id_type=MESH,
                ).start()
            sent[link] += slots

    def share(event):
        base, slots = place(event)
        ref = arr.at[pl.ds(base, slots), :, pl.ds(own_col, HD)]
        pltpu.make_async_remote_copy(
            src_ref=ref,
            dst_ref=ref,
            send_sem=kv_send.at[0],
            recv_sem=kv_recv.at[PLACE[event]],
            device_id=other_core,
            device_id_type=MESH,
        ).start()

    def shared_wait(event):
        _, slots = place(event)
        ref = arr.at[pl.ds(0, slots), :, pl.ds(QC, HD)]
        pltpu.make_async_copy(ref, ref, kv_recv.at[PLACE[event]]).wait()

    def send_cache(row):
        pltpu.make_async_remote_copy(
            src_ref=cache.at[pl.ds(row, 1)],
            dst_ref=cache_other.at[pl.ds(row, 1)],
            send_sem=cache_send.at[0],
            recv_sem=cache_recv.at[0],
            device_id=other_core,
            device_id_type=MESH,
        ).start()

    def prepare():
        for copy in prep:
            copy.wait()
        slots = jnp.broadcast_to(slot_row[...], (NB, NB))
        by_bucket = jnp.transpose(slots)
        hit = by_bucket == lax.broadcasted_iota(jnp.int32, (NB, NB), 1)
        bucket = lax.broadcasted_iota(jnp.int32, (NB, NB), 0)
        inv_row[...] = jnp.max(jnp.where(hit, bucket, 0), axis=0, keepdims=True)
        move = pltpu.make_async_copy(inv_row, inv, prep_sem.at[3])
        move.start()

        def squares(j, total):
            part = hid[:, pl.ds(pl.multiple_of(j * 512, 512), 512)].astype(jnp.float32)
            return total + jnp.sum(part * part, axis=-1, keepdims=True)

        total = lax.fori_loop(0, D // 512, squares, jnp.zeros((M, 1), jnp.float32))
        factor = lax.rsqrt(total * (1.0 / D) + norm_eps)

        def turn(j, carry):
            cols = pl.ds(pl.multiple_of(j * 128, 128), 128)
            part = hid[:, cols].astype(jnp.float32) * factor * gain[:, cols]
            part = part.astype(jnp.bfloat16).astype(jnp.float32)
            part = jnp.transpose(part).astype(jnp.bfloat16)
            turned[pl.ds(j * 4, 4)] = part.reshape(4, BROWS, M)
            return carry

        lax.fori_loop(0, D // 128, turn, 0)
        move.wait()

        def pick(j, carry):
            rows = [turned[inv[0, j * 4 + i]] for i in range(4)]
            part = jnp.concatenate(rows, axis=0).astype(jnp.float32)
            lhs[j] = jnp.transpose(part).astype(jnp.bfloat16)
            return carry

        lax.fori_loop(0, NB // 4, pick, 0)

        row = lax.broadcasted_iota(jnp.int32, (M, HD), 0)
        position = jnp.zeros((M, HD), jnp.int32)
        for b in range(ROWS):
            for s in range(STEPS):
                position = jnp.where(row == s * ROWS + b, len_ref[b] + s, position)
        angle = position.astype(jnp.float32) * freq_ref[...]
        lane = lax.broadcasted_iota(jnp.int32, (M, HD), 1)
        cos_ref[...] = jnp.cos(angle)
        sine = jnp.sin(angle)
        sin_ref[...] = jnp.where(lane < HD // 2, -sine, sine)
        proj[...] = jnp.zeros_like(proj)

    def multiply(base, column, width):
        rows = arr[pl.ds(base, 4), :, pl.ds(column, width)].reshape(4 * BROWS, width)
        return jnp.dot(lhs[base // 4], rows, preferred_element_type=jnp.float32)

    def add_own(base):
        base = pl.multiple_of(base, 4)
        proj[:, :QC] += multiply(base, 0, QC)
        proj[:, pl.ds(own_col, HD)] += multiply(base, own_col, HD)

    def add_other(base):
        base = pl.multiple_of(base, 4)
        proj[:, pl.ds(other_col, HD)] += multiply(base, other_col, HD)

    def unit_of(event):
        kind, item = event[0], event[1]
        unit = ITEMS[item][0]
        if kind in ("entry", "pair"):
            return (kind, unit)
        way = event[2] if kind == "late" else kind
        side = 1 if kind == "late" else event[2]
        far = way in ("up2", "down2")
        return ("far" if far else way, side, unit)

    missing = {}
    for event in EVENTS:
        missing.setdefault(unit_of(event), set()).add(event)
    base_of = {}
    ready = []
    for name, members in missing.items():
        some = next(event for event in EVENTS if event in members)
        kind = some[0]
        if kind == "entry":
            base_of[name] = unit_base(name[1], z, p)
        elif kind == "pair":
            base_of[name] = unit_base(name[1], z, 1 - p)
        else:
            z_of = {"up1": up_z, "down1": down_z, "far": far_z}[name[0]]
            base_of[name] = unit_base(name[2], z_of, (p + name[1]) % 2)
    members_of = {name: sorted(events, key=PLACE.get) for name, events in missing.items()}
    waiting_other = []
    prepared = False
    cache_rows = iter(range(ROWS))
    for step, event in enumerate(EVENTS):
        wait_for(event)
        forward(event)
        share(event)
        if event == ("entry", 4):
            for unit in (4, 5, 6, 7):
                send_unit(unit)
        name = unit_of(event)
        missing[name].remove(event)
        if not missing[name]:
            ready.append(name)
        if step == 8:
            prepare()
            prepared = True
        if step >= 12:
            row = next(cache_rows, None)
            if row is not None:
                send_cache(row)
        if prepared:
            for name in ready:
                add_own(base_of[name])
                waiting_other.append(name)
            ready = []
            while len(waiting_other) > 6:
                name = waiting_other.pop(0)
                for member in members_of[name]:
                    shared_wait(member)
                add_other(base_of[name])
    for name in waiting_other:
        for member in members_of[name]:
            shared_wait(member)
        add_other(base_of[name])

    for link, slots in sent.items():
        wait_bytes(slots, link_sem.at[link_index[link]])
    wait_bytes(30, stage_sem.at[0])
    everything = arr.at[:, :, pl.ds(QC, HD)]
    pltpu.make_async_copy(everything, everything, kv_send.at[0]).wait()
    pltpu.make_async_copy(cache, cache, cache_send.at[0]).wait()
    pltpu.make_async_copy(cache, cache, cache_recv.at[0]).wait()


def attend_kernel(
    slot_ref,
    len_ref,
    arr,
    proj,
    cos_ref,
    sin_ref,
    cache,
    cache_other,
    served,
    context,
    kv,
    queries,
    scores,
    probs,
    outs,
    kv_sem,
    served_sem,
):
    c = lax.axis_index("tensor") % 2
    groups = 4
    per = ROWS // groups

    def load(group, half):
        rows = pl.ds(group * per, per)
        return pltpu.make_async_copy(
            (cache, cache_other)[half].at[rows], kv.at[rows, pl.ds(half * HALF, HALF)], kv_sem.at[group, half]
        )

    for group in range(groups):
        for half in range(2):
            load(group, half).start()

    def install(b):
        pltpu.make_async_copy(
            arr.at[slot_ref[b]], served.at[0, pl.ds(pl.multiple_of(b * BROWS, BROWS), BROWS)], served_sem.at[0]
        ).start()

    def rotate(block):
        return (block * cos_ref[...] + pltpu.roll(block, HD // 2, 1) * sin_ref[...]).astype(jnp.bfloat16)

    for head in range(HEADS):
        turned = rotate(proj[:, pl.ds(head * HD, HD)]).astype(jnp.float32)
        for s in range(STEPS):
            queries[:, s * HEADS + head, :] = turned[s * ROWS : (s + 1) * ROWS]
    keys_new = rotate(proj[:, pl.ds(QC, HD)]).astype(jnp.float32).reshape(STEPS, ROWS, 1, HD)
    values_new = proj[:, pl.ds(QC + HD, HD)].astype(jnp.bfloat16).astype(jnp.float32)
    values_new = values_new.reshape(STEPS, ROWS, 1, HD)

    scale_factor = HD ** (-0.5)
    column = lax.broadcasted_iota(jnp.int32, (1, LEN), 1)
    position = jnp.where(column < HALF, column + c * HALF, column - c * HALF)
    dims = (((1,), (1,)), ((), ()))

    for group in range(groups):
        for half in range(2):
            load(group, half).wait()

        def score(i, carry):
            b = group * per + i
            for k in range(NB // ROWS):
                install(b * (NB // ROWS) + k)
            found = lax.dot_general(
                queries[b].astype(jnp.bfloat16), kv[b, :, :HD], dims, preferred_element_type=jnp.float32
            )
            scores[b] = jnp.where(position < len_ref[b], found * scale_factor, masked_score)
            return carry

        lax.fori_loop(0, per, score, 0, unroll=2)

    query = queries[...]
    fresh = [jnp.sum(query * keys_new[s], axis=-1, keepdims=True) * scale_factor for s in range(STEPS)]
    step = lax.broadcasted_iota(jnp.int32, (ROWS, STEPS * HEADS, 1), 1) // HEADS
    fresh[1] = jnp.where(step >= 1, fresh[1], masked_score)
    found = scores[...]
    peaks = jnp.maximum(jnp.max(found, axis=-1, keepdims=True), jnp.maximum(fresh[0], fresh[1]))
    weights = jnp.exp(found - peaks).astype(jnp.bfloat16)
    probs[...] = weights
    total = jnp.sum(weights.astype(jnp.float32), axis=-1, keepdims=True)
    fresh = [jnp.exp(one - peaks).astype(jnp.bfloat16).astype(jnp.float32) for one in fresh]
    total = total + fresh[0] + fresh[1]
    extra = fresh[0] * values_new[0] + fresh[1] * values_new[1]

    def gather(b, carry):
        outs[b] = jnp.dot(probs[b], kv[b, :, HD:], preferred_element_type=jnp.float32)
        return carry

    lax.fori_loop(0, ROWS, gather, 0, unroll=4)
    outs[...] = (outs[...] + extra) / total
    for head in range(HEADS):
        for s in range(STEPS):
            context[pl.ds(s * ROWS, ROWS), pl.ds(head * HD, HD)] = outs[:, s * HEADS + head, :].astype(jnp.bfloat16)
    pltpu.make_async_copy(served, served, served_sem.at[0]).wait()


def on_device(hidden_in, norm_gain, qkv_buckets, bucket_slot, kv_cache, cache_len):
    any_space = pl.BlockSpec(memory_space=pl.ANY)
    vmem = pl.BlockSpec(memory_space=pltpu.VMEM)
    smem = pl.BlockSpec(memory_space=pltpu.SMEM)
    freqs = rope_base ** (-2.0 * jnp.arange(HD // 2, dtype=jnp.float32) / HD)
    freqs = jnp.concatenate([freqs, freqs]).reshape(1, HD)
    dma = pltpu.SemaphoreType.DMA
    arr, proj, cosine, sine, cache_other = pl.pallas_call(
        gather_kernel,
        out_shape=[
            pltpu.VMEM((NB, BROWS, COLS), jnp.bfloat16),
            pltpu.VMEM((M, COLS), jnp.float32),
            pltpu.VMEM((M, HD), jnp.float32),
            pltpu.VMEM((M, HD), jnp.float32),
            jax.ShapeDtypeStruct(kv_cache.shape, kv_cache.dtype),
        ],
        in_specs=[any_space] * 5 + [vmem, smem],
        out_specs=[vmem] * 4 + [any_space],
        scratch_shapes=[
            pltpu.VMEM((M, D), jnp.bfloat16),
            pltpu.VMEM((1, D), jnp.float32),
            pltpu.VMEM((1, NB), jnp.int32),
            pltpu.VMEM((1, NB), jnp.int32),
            pltpu.SMEM((1, NB), jnp.int32),
            pltpu.VMEM((NB, BROWS, M), jnp.bfloat16),
            pltpu.VMEM((NB // 4, M, 4 * BROWS), jnp.bfloat16),
            dma((1,)),
            dma((4,)),
            dma((2,)),
            dma((len(EVENTS),)),
            dma((16,)),
            dma((3,)),
            dma((1,)),
            dma((1,)),
            dma((len(EVENTS),)),
            dma((1,)),
            dma((1,)),
        ],
        compiler_params=pltpu.CompilerParams(
            collective_id=0, has_side_effects=True, vmem_limit_bytes=10 * 2**20
        ),
        name="gather_and_project",
    )(
        hidden_in.reshape(M, D),
        norm_gain.reshape(1, D),
        qkv_buckets,
        bucket_slot.reshape(1, NB),
        kv_cache,
        freqs,
        cache_len,
    )
    served, context = pl.pallas_call(
        attend_kernel,
        out_shape=[
            jax.ShapeDtypeStruct((1, D, COLS), jnp.bfloat16),
            jax.ShapeDtypeStruct((M, QC), jnp.bfloat16),
        ],
        in_specs=[smem, smem] + [vmem] * 4 + [any_space] * 2,
        out_specs=[any_space, vmem],
        scratch_shapes=[
            pltpu.VMEM((ROWS, LEN, 2 * HD), jnp.bfloat16),
            pltpu.VMEM((ROWS, STEPS * HEADS, HD), jnp.float32),
            pltpu.VMEM((ROWS, STEPS * HEADS, LEN), jnp.float32),
            pltpu.VMEM((ROWS, STEPS * HEADS, LEN), jnp.bfloat16),
            pltpu.VMEM((ROWS, STEPS * HEADS, HD), jnp.float32),
            dma((4, 2)),
            dma((1,)),
        ],
        compiler_params=pltpu.CompilerParams(vmem_limit_bytes=24 * 2**20),
        name="attend_and_install",
    )(bucket_slot, cache_len, arr, proj, cosine, sine, kv_cache, cache_other)
    return context.reshape(STEPS, ROWS, QC), served


def solution(mesh):
    in_specs = (
        P(None, "replica", None),
        P(),
        P(("replica", "tensor"), None, None),
        P(),
        P("replica", "tensor", None),
        P("replica"),
    )
    out_specs = (P(None, "replica", "tensor"), P("tensor", None, None))
    return jax.shard_map(
        on_device, mesh=mesh, in_specs=in_specs, out_specs=out_specs, check_vma=False
    )
```

```python
import functools
import heapq
import itertools

import jax
import jax.numpy as jnp
import numpy as np
from jax import lax
from jax.experimental import pallas as pl
from jax.experimental.pallas import tpu as pltpu
from jax.sharding import PartitionSpec as P

QH = 64
KVH = 8
HD = 128
D = 8192
LEN = 2048
STEPS = 2
BROWS = 32
NB = 256
N_TENSOR = 16
N_REPLICA = 8
ROWS = 16
M = STEPS * ROWS
QC = 512
OWN = QC + HD
COLS = QC + 2 * HD
HEADS = QC // HD
HALF = LEN // 2

rope_base = 500000.0
norm_eps = 1e-05
masked_score = -1e30

MESH = pl.DeviceIdType.MESH

UNITS = ((0, 0), (1, 0), (3, 0), (0, 1), (1, 1), (3, 1), (2, 0), (2, 1))
ITEMS = ((0, 0, 2), (0, 2, 2)) + tuple((u, 0, 4) for u in range(1, 8))
PAIR_FIRST = frozenset((0, 2, 4, 5, 7))


def event_order():
    per_slot, hop = 0.87, 0.8
    entry = (0.7, 0.7, 5.0, 5.0, 5.5, 10.0, 11.0, 15.0, 16.0)
    links = ("pair", "up", "down")
    free = dict.fromkeys(links, 0.0)
    queue = {link: [] for link in links}
    count = itertools.count()
    events = [(entry[i], next(count), ("entry", i)) for i in range(len(ITEMS))]
    heapq.heapify(events)
    order = []
    while events:
        now, _, event = heapq.heappop(events)
        if event is not None:
            order.append(event)
            for link, arrival, slots in forwards(event):
                queue[link].append((arrival, slots))
        for link in links:
            if queue[link] and free[link] <= now + 1e-9:
                arrival, slots = queue[link].pop(0)
                free[link] = now + slots * per_slot
                heapq.heappush(events, (free[link] + hop, next(count), arrival))
                heapq.heappush(events, (free[link], next(count), None))
    return order


def forwards(event):
    kind, item = event[0], event[1]
    slots = ITEMS[item][2]
    sends = []
    if kind == "entry":
        sends += [("pair", ("pair", item), slots)]
        sends += [("up", ("up1", item, 0), slots), ("down", ("down1", item, 0), slots)]
    elif kind == "pair" and item in PAIR_FIRST:
        sends += [("up", ("up1", item, 1), slots), ("down", ("down1", item, 1), slots)]
    elif kind in ("up1", "down1"):
        link = kind[:-1]
        sends += [(link, (link + "2", item, event[2]), slots // 2)]
        if item not in PAIR_FIRST:
            sends += [("pair", ("late", item, kind), slots)]
    elif kind in ("up2", "down2") and item not in PAIR_FIRST:
        sends += [("pair", ("late", item, kind), slots // 2)]
    return sends


EVENTS = event_order()
PLACE = {event: i for i, event in enumerate(EVENTS)}


def gather_kernel(
    hid_hbm,
    gain_hbm,
    buckets,
    slot_hbm,
    cache,
    freq_ref,
    len_hbm,
    arr,
    proj,
    cos_ref,
    sin_ref,
    kv,
    hid,
    gain,
    slot_row,
    inv_row,
    inv,
    len_ref,
    factor,
    turned,
    lhs,
    prep_sem,
    own_sem,
    recv_sem,
    recv_kv_sem,
    entry_sem,
    entry_kv_sem,
    link_sem,
    stage_sem,
    kv_send,
    kv_recv,
    cache_send,
    cache_recv,
):
    r = lax.axis_index("replica")
    t = lax.axis_index("tensor")
    z, p = r // 2, r % 2
    x, h, c = t // 4, (t // 2) % 2, t % 2
    other_core = (r, x * 4 + h * 2 + (1 - c))
    next_replica = {
        "pair": z * 2 + (1 - p),
        "up": ((z + 1) % 4) * 2 + p,
        "down": ((z + 3) % 4) * 2 + p,
    }
    target = {link: (replica, t) for link, replica in next_replica.items()}
    across = {link: (replica, other_core[1]) for link, replica in next_replica.items()}
    own_col = pl.multiple_of(QC + HD * c, HD)
    other_col = pl.multiple_of(QC + HD * (1 - c), HD)

    prep = [
        pltpu.make_async_copy(hid_hbm, hid, prep_sem.at[0]),
        pltpu.make_async_copy(gain_hbm, gain, prep_sem.at[1]),
        pltpu.make_async_copy(slot_hbm, slot_row, prep_sem.at[2]),
        pltpu.make_async_copy(len_hbm, len_ref, prep_sem.at[3]),
    ]
    for copy in prep:
        copy.start()

    def chip(dx, dh, core):
        return (z * 2 + (p + dh) % 2, ((x + dx) % 4) * 4 + ((h + dh) % 2) * 2 + core)

    barrier = pltpu.get_barrier_semaphore()
    peers = [other_core] + list(target.values()) + list(across.values())
    peers += [chip(dx, dh, core) for dx, dh in UNITS[1:] for core in range(2)]
    for peer in peers:
        pl.semaphore_signal(barrier, inc=1, device_id=peer, device_id_type=MESH)
    pl.semaphore_wait(barrier, len(peers))

    mine = (r * N_TENSOR + t) * 2
    sent = {"pair": 0, "up": 0, "down": 0}
    link_index = {"pair": 0, "up": 1, "down": 2}

    def parts(base, slots):
        rows = pl.ds(base, slots)
        return arr.at[rows, :, pl.ds(own_col, HD)], arr.at[rows, :, pl.ds(0, QC)]

    def bucket_parts(x_to, h_to, core):
        group = x_to * 2 + h_to
        query = pl.multiple_of((group * 2 + core) * QC, QC)
        key = pl.multiple_of(QH * HD + core * (KVH * HD) + group * HD, HD)
        return buckets.at[:, :, pl.ds(key, HD)], buckets.at[:, :, pl.ds(query, QC)]

    def own_columns(core):
        return pl.ds(pl.multiple_of(QC + HD * core, HD), HD), pl.ds(0, QC)

    def send_mine(x_to, h_to, core, dst, send_sem, recv_sems):
        for src, cols, recv in zip(bucket_parts(x_to, h_to, core), own_columns(core), recv_sems):
            pltpu.make_async_remote_copy(
                src_ref=src,
                dst_ref=arr.at[pl.ds(mine, 2), :, cols],
                send_sem=send_sem,
                recv_sem=recv,
                device_id=dst,
                device_id_type=MESH,
            ).start()

    def send_unit(unit):
        dx, dh = UNITS[unit]
        x_to, h_to, p_to = (x + 4 - dx) % 4, (h + dh) % 2, (p + dh) % 2
        sems = (entry_kv_sem.at[2 * unit + c], entry_sem.at[2 * unit + c])
        for core in range(2):
            dst = (z * 2 + p_to, x_to * 4 + h_to * 2 + core)
            send_mine(x_to, h_to, core, dst, stage_sem.at[0], sems)

    def wait_bytes(slots, sem, width=OWN):
        ref = arr.at[pl.ds(0, slots), :, pl.ds(0, width)]
        pltpu.make_async_copy(ref, ref, sem).wait()

    for item, core in ((0, c), (1, 1 - c)):
        for link, arrival, slots in forwards(("entry", item)):
            place_of = PLACE[arrival]
            dst = (target, across)[item][link]
            sems = (recv_kv_sem.at[place_of], recv_sem.at[place_of])
            send_mine(x, h, core, dst, link_sem.at[link_index[link]], sems)
            sent[link] += slots
    own_copies = []
    for src, dst in zip(bucket_parts(x, h, c), parts(mine, 2)):
        copy = pltpu.make_async_copy(src, dst, own_sem.at[len(own_copies)])
        copy.start()
        own_copies.append(copy)
    send_mine(x, h, 1 - c, other_core, stage_sem.at[0], (entry_kv_sem.at[0], entry_sem.at[0]))
    for unit in (1, 2, 3):
        send_unit(unit)

    def unit_base(unit, z_of, p_of):
        dx, dh = UNITS[unit]
        source = z_of * 2 + (p_of + dh) % 2
        return source * 32 + ((x + dx) % 4) * 8 + ((h + dh) % 2) * 4

    up_z, down_z, far_z = (z + 3) % 4, (z + 1) % 4, (z + 2) % 4

    def place(event):
        kind, item = event[0], event[1]
        unit, first, slots = ITEMS[item]
        if kind == "entry":
            z_of, p_of = z, p
        elif kind == "pair":
            z_of, p_of = z, 1 - p
        else:
            way = event[2] if kind == "late" else kind
            z_of = {"up1": up_z, "down1": down_z, "up2": far_z, "down2": far_z}[way]
            if kind == "late":
                p_of = 1 - p
            else:
                p_of = (p + event[2]) % 2
            if way in ("up2", "down2"):
                slots = slots // 2
                if way == "down2":
                    first = first + slots
        base = unit_base(unit, z_of, p_of)
        if unit == 0:
            own_half = 2 * c if item == 0 else 2 * (1 - c)
            base = base + own_half + (first - ITEMS[item][1])
        else:
            base = base + first
        return base, slots

    def wait_for(event, part):
        width = (HD, QC)[part]
        if event == ("entry", 0):
            own_copies[part].wait()
        elif event == ("entry", 1):
            wait_bytes(2, (entry_kv_sem, entry_sem)[part].at[0], width)
        elif event[0] == "entry":
            unit = ITEMS[event[1]][0]
            for core in range(2):
                wait_bytes(2, (entry_kv_sem, entry_sem)[part].at[2 * unit + core], width)
        else:
            wait_bytes(place(event)[1], (recv_kv_sem, recv_sem)[part].at[PLACE[event]], width)

    def forward(event, part):
        if event in (("entry", 0), ("entry", 1)):
            return
        base, _ = place(event)
        for link, arrival, slots in forwards(event):
            start = base
            if arrival[0] == "down2":
                start = base + slots
            ref = parts(start, slots)[part]
            pltpu.make_async_remote_copy(
                src_ref=ref,
                dst_ref=ref,
                send_sem=link_sem.at[link_index[link]],
                recv_sem=(recv_kv_sem, recv_sem)[part].at[PLACE[arrival]],
                device_id=target[link],
                device_id_type=MESH,
            ).start()
            if part == 1:
                sent[link] += slots

    def share(event):
        base, slots = place(event)
        ref = arr.at[pl.ds(base, slots), :, pl.ds(own_col, HD)]
        pltpu.make_async_remote_copy(
            src_ref=ref,
            dst_ref=ref,
            send_sem=kv_send.at[0],
            recv_sem=kv_recv.at[PLACE[event]],
            device_id=other_core,
            device_id_type=MESH,
        ).start()

    def shared_wait(event):
        _, slots = place(event)
        ref = arr.at[pl.ds(0, slots), :, pl.ds(QC, HD)]
        pltpu.make_async_copy(ref, ref, kv_recv.at[PLACE[event]]).wait()

    own_half = pl.ds(pl.multiple_of(c * HALF, HALF), HALF)

    def send_cache(row):
        pltpu.make_async_copy(cache.at[row], kv.at[row, own_half], cache_send.at[1]).start()
        pltpu.make_async_remote_copy(
            src_ref=cache.at[row],
            dst_ref=kv.at[row, own_half],
            send_sem=cache_send.at[0],
            recv_sem=cache_recv.at[0],
            device_id=other_core,
            device_id_type=MESH,
        ).start()

    def squares(j, total):
        part = hid[:, pl.ds(pl.multiple_of(j * 512, 512), 512)].astype(jnp.float32)
        return total + jnp.sum(part * part, axis=-1, keepdims=True)

    def turn(j, carry):
        cols = pl.ds(pl.multiple_of(j * 128, 128), 128)
        part = hid[:, cols].astype(jnp.float32) * factor[...] * gain[:, cols]
        part = part.astype(jnp.bfloat16).astype(jnp.float32)
        part = jnp.transpose(part).astype(jnp.bfloat16)
        turned[pl.ds(j * 4, 4)] = part.reshape(4, BROWS, M)
        return carry

    def pick(j, carry):
        rows = [turned[inv[0, j * 4 + i]] for i in range(4)]
        part = jnp.concatenate(rows, axis=0).astype(jnp.float32)
        lhs[j] = jnp.transpose(part).astype(jnp.bfloat16)
        return carry

    move = pltpu.make_async_copy(inv_row, inv, prep_sem.at[4])

    def find_slots():
        for copy in prep:
            copy.wait()
        slots = jnp.broadcast_to(slot_row[...], (NB, NB))
        by_bucket = jnp.transpose(slots)
        hit = by_bucket == lax.broadcasted_iota(jnp.int32, (NB, NB), 1)
        bucket = lax.broadcasted_iota(jnp.int32, (NB, NB), 0)
        inv_row[...] = jnp.max(jnp.where(hit, bucket, 0), axis=0, keepdims=True)
        move.start()

    def find_factor():
        total = lax.fori_loop(0, D // 512, squares, jnp.zeros((M, 1), jnp.float32))
        factor[...] = jnp.broadcast_to(lax.rsqrt(total * (1.0 / D) + norm_eps), (M, HD))
        move.wait()

    def find_angles():
        row = lax.broadcasted_iota(jnp.int32, (M, HD), 0)
        position = jnp.zeros((M, HD), jnp.int32)
        for b in range(ROWS):
            for s in range(STEPS):
                position = jnp.where(row == s * ROWS + b, len_ref[b] + s, position)
        angle = position.astype(jnp.float32) * freq_ref[...]
        lane = lax.broadcasted_iota(jnp.int32, (M, HD), 1)
        cos_ref[...] = jnp.cos(angle)
        sine = jnp.sin(angle)
        sin_ref[...] = jnp.where(lane < HD // 2, -sine, sine)
        proj[...] = jnp.zeros_like(proj)

    slices = 8
    span = D // 128 // slices
    prepare = [find_slots, find_factor, find_angles]
    for body in (turn, pick):
        for i in range(slices):
            prepare.append(functools.partial(lax.fori_loop, i * span, (i + 1) * span, body, 0))
    prepare = iter(prepare)

    def multiply(base, column, width):
        rows = arr[pl.ds(base, 4), :, pl.ds(column, width)].reshape(4 * BROWS, width)
        return jnp.dot(lhs[base // 4], rows, preferred_element_type=jnp.float32)

    def add_own(base):
        base = pl.multiple_of(base, 4)
        proj[:, :QC] += multiply(base, 0, QC)
        proj[:, pl.ds(own_col, HD)] += multiply(base, own_col, HD)

    def add_other(base):
        base = pl.multiple_of(base, 4)
        proj[:, pl.ds(other_col, HD)] += multiply(base, other_col, HD)

    def unit_of(event):
        kind, item = event[0], event[1]
        unit = ITEMS[item][0]
        if kind in ("entry", "pair"):
            return (kind, unit)
        way = event[2] if kind == "late" else kind
        side = 1 if kind == "late" else event[2]
        far = way in ("up2", "down2")
        return ("far" if far else way, side, unit)

    missing = {}
    for event in EVENTS:
        missing.setdefault(unit_of(event), set()).add(event)
    base_of = {}
    ready = []
    for name, members in missing.items():
        some = next(event for event in EVENTS if event in members)
        kind = some[0]
        if kind == "entry":
            base_of[name] = unit_base(name[1], z, p)
        elif kind == "pair":
            base_of[name] = unit_base(name[1], z, 1 - p)
        else:
            z_of = {"up1": up_z, "down1": down_z, "far": far_z}[name[0]]
            base_of[name] = unit_base(name[2], z_of, (p + name[1]) % 2)
    members_of = {name: sorted(events, key=PLACE.get) for name, events in missing.items()}
    waiting_other = []
    prepared = False
    cache_rows = iter(range(ROWS))
    for step, event in enumerate(EVENTS):
        wait_for(event, 0)
        forward(event, 0)
        share(event)
        wait_for(event, 1)
        forward(event, 1)
        if event == ("entry", 4):
            for unit in (4, 5, 6, 7):
                send_unit(unit)
        name = unit_of(event)
        missing[name].remove(event)
        if not missing[name]:
            ready.append(name)
        if step >= 20 and not prepared:
            work = next(prepare, None)
            if work is None:
                prepared = True
            else:
                work()
        if step >= 12:
            row = next(cache_rows, None)
            if row is not None:
                send_cache(row)
        if prepared:
            for name in ready[:2]:
                add_own(base_of[name])
                waiting_other.append(name)
            ready = ready[2:]
            while len(waiting_other) > 2:
                name = waiting_other.pop(0)
                for member in members_of[name]:
                    shared_wait(member)
                add_other(base_of[name])
    for name in ready:
        add_own(base_of[name])
        waiting_other.append(name)
    for name in waiting_other:
        for member in members_of[name]:
            shared_wait(member)
        add_other(base_of[name])

    for link, slots in sent.items():
        wait_bytes(slots, link_sem.at[link_index[link]])
    wait_bytes(30, stage_sem.at[0])
    everything = arr.at[:, :, pl.ds(QC, HD)]
    pltpu.make_async_copy(everything, everything, kv_send.at[0]).wait()
    pltpu.make_async_copy(cache, cache, cache_send.at[0]).wait()
    pltpu.make_async_copy(cache, cache, cache_send.at[1]).wait()
    pltpu.make_async_copy(cache, cache, cache_recv.at[0]).wait()


def attend_kernel(
    slot_ref,
    len_ref,
    arr,
    proj,
    cos_ref,
    sin_ref,
    kv,
    served,
    context,
    queries,
    scores,
    probs,
    outs,
    served_sem,
):
    def install(b):
        pltpu.make_async_copy(
            arr.at[slot_ref[b]], served.at[0, pl.ds(pl.multiple_of(b * BROWS, BROWS), BROWS)], served_sem.at[0]
        ).start()

    def rotate(block):
        return (block * cos_ref[...] + pltpu.roll(block, HD // 2, 1) * sin_ref[...]).astype(jnp.bfloat16)

    for head in range(HEADS):
        turned = rotate(proj[:, pl.ds(head * HD, HD)]).astype(jnp.float32)
        for s in range(STEPS):
            queries[:, s * HEADS + head, :] = turned[s * ROWS : (s + 1) * ROWS]
    keys_new = rotate(proj[:, pl.ds(QC, HD)]).astype(jnp.float32).reshape(STEPS, ROWS, 1, HD)
    values_new = proj[:, pl.ds(QC + HD, HD)].astype(jnp.bfloat16).astype(jnp.float32)
    values_new = values_new.reshape(STEPS, ROWS, 1, HD)

    scale_factor = HD ** (-0.5)
    position = lax.broadcasted_iota(jnp.int32, (1, LEN), 1)
    dims = (((1,), (1,)), ((), ()))

    def score(b, carry):
        for k in range(NB // ROWS):
            install(b * (NB // ROWS) + k)
        found = lax.dot_general(
            queries[b].astype(jnp.bfloat16), kv[b, :, :HD], dims, preferred_element_type=jnp.float32
        )
        scores[b] = jnp.where(position < len_ref[b], found * scale_factor, masked_score)
        return carry

    lax.fori_loop(0, ROWS, score, 0, unroll=2)

    query = queries[...]
    fresh = [jnp.sum(query * keys_new[s], axis=-1, keepdims=True) * scale_factor for s in range(STEPS)]
    step = lax.broadcasted_iota(jnp.int32, (ROWS, STEPS * HEADS, 1), 1) // HEADS
    fresh[1] = jnp.where(step >= 1, fresh[1], masked_score)
    found = scores[...]
    peaks = jnp.maximum(jnp.max(found, axis=-1, keepdims=True), jnp.maximum(fresh[0], fresh[1]))
    weights = jnp.exp(found - peaks).astype(jnp.bfloat16)
    probs[...] = weights
    total = jnp.sum(weights.astype(jnp.float32), axis=-1, keepdims=True)
    fresh = [jnp.exp(one - peaks).astype(jnp.bfloat16).astype(jnp.float32) for one in fresh]
    total = total + fresh[0] + fresh[1]
    extra = fresh[0] * values_new[0] + fresh[1] * values_new[1]

    def gather(b, carry):
        outs[b] = jnp.dot(probs[b], kv[b, :, HD:], preferred_element_type=jnp.float32)
        return carry

    lax.fori_loop(0, ROWS, gather, 0, unroll=4)
    outs[...] = (outs[...] + extra) / total
    for head in range(HEADS):
        for s in range(STEPS):
            context[pl.ds(s * ROWS, ROWS), pl.ds(head * HD, HD)] = outs[:, s * HEADS + head, :].astype(jnp.bfloat16)
    pltpu.make_async_copy(served, served, served_sem.at[0]).wait()


def on_device(hidden_in, norm_gain, qkv_buckets, bucket_slot, kv_cache, cache_len):
    any_space = pl.BlockSpec(memory_space=pl.ANY)
    vmem = pl.BlockSpec(memory_space=pltpu.VMEM)
    smem = pl.BlockSpec(memory_space=pltpu.SMEM)
    freqs = rope_base ** (-2.0 * jnp.arange(HD // 2, dtype=jnp.float32) / HD)
    freqs = jnp.concatenate([freqs, freqs]).reshape(1, HD)
    dma = pltpu.SemaphoreType.DMA
    in_hbm = functools.partial(pltpu.with_memory_space_constraint, memory_space=pltpu.HBM)
    in_vmem = functools.partial(pltpu.with_memory_space_constraint, memory_space=pltpu.VMEM)
    arr, proj, cosine, sine, kv = pl.pallas_call(
        gather_kernel,
        out_shape=[
            pltpu.VMEM((NB, BROWS, COLS), jnp.bfloat16),
            pltpu.VMEM((M, COLS), jnp.float32),
            pltpu.VMEM((M, HD), jnp.float32),
            pltpu.VMEM((M, HD), jnp.float32),
            pltpu.VMEM((ROWS, LEN, 2 * HD), jnp.bfloat16),
        ],
        in_specs=[any_space] * 5 + [vmem, any_space],
        out_specs=[vmem] * 5,
        scratch_shapes=[
            pltpu.VMEM((M, D), jnp.bfloat16),
            pltpu.VMEM((1, D), jnp.float32),
            pltpu.VMEM((1, NB), jnp.int32),
            pltpu.VMEM((1, NB), jnp.int32),
            pltpu.SMEM((1, NB), jnp.int32),
            pltpu.SMEM((ROWS,), jnp.int32),
            pltpu.VMEM((M, HD), jnp.float32),
            pltpu.VMEM((NB, BROWS, M), jnp.bfloat16),
            pltpu.VMEM((NB // 4, M, 4 * BROWS), jnp.bfloat16),
            dma((5,)),
            dma((2,)),
            dma((len(EVENTS),)),
            dma((len(EVENTS),)),
            dma((16,)),
            dma((16,)),
            dma((3,)),
            dma((1,)),
            dma((1,)),
            dma((len(EVENTS),)),
            dma((2,)),
            dma((1,)),
        ],
        compiler_params=pltpu.CompilerParams(
            collective_id=0, has_side_effects=True, vmem_limit_bytes=10 * 2**20
        ),
        name="gather_and_project",
    )(
        in_hbm(hidden_in.reshape(M, D)),
        in_hbm(norm_gain.reshape(1, D)),
        in_hbm(qkv_buckets),
        in_hbm(bucket_slot.reshape(1, NB)),
        in_hbm(kv_cache),
        freqs,
        in_hbm(cache_len),
    )
    served, context = pl.pallas_call(
        attend_kernel,
        out_shape=[
            pltpu.HBM((1, D, COLS), jnp.bfloat16),
            jax.ShapeDtypeStruct((M, QC), jnp.bfloat16),
        ],
        in_specs=[smem, smem] + [vmem] * 5,
        out_specs=[any_space, vmem],
        scratch_shapes=[
            pltpu.VMEM((ROWS, STEPS * HEADS, HD), jnp.float32),
            pltpu.VMEM((ROWS, STEPS * HEADS, LEN), jnp.float32),
            pltpu.VMEM((ROWS, STEPS * HEADS, LEN), jnp.bfloat16),
            pltpu.VMEM((ROWS, STEPS * HEADS, HD), jnp.float32),
            dma((1,)),
        ],
        compiler_params=pltpu.CompilerParams(vmem_limit_bytes=12 * 2**20),
        name="attend_and_install",
    )(in_hbm(bucket_slot), in_hbm(cache_len), in_vmem(arr), in_vmem(proj), in_vmem(cosine), in_vmem(sine), in_vmem(kv))
    return context.reshape(STEPS, ROWS, QC), served


def solution(mesh):
    in_specs = (
        P(None, "replica", None),
        P(),
        P(("replica", "tensor"), None, None),
        P(),
        P("replica", "tensor", None),
        P("replica"),
    )
    out_specs = (P(None, "replica", "tensor"), P("tensor", None, None))
    return jax.shard_map(
        on_device, mesh=mesh, in_specs=in_specs, out_specs=out_specs, check_vma=False
    )
```

```python
import functools
import heapq
import itertools

import jax
import jax.numpy as jnp
import numpy as np
from jax import lax
from jax.experimental import pallas as pl
from jax.experimental.pallas import tpu as pltpu
from jax.sharding import PartitionSpec as P

QH = 64
KVH = 8
HD = 128
D = 8192
LEN = 2048
STEPS = 2
BROWS = 32
NB = 256
N_TENSOR = 16
N_REPLICA = 8
ROWS = 16
M = STEPS * ROWS
QC = 512
OWN = QC + HD
COLS = QC + 2 * HD
HEADS = QC // HD
HALF = LEN // 2

rope_base = 500000.0
norm_eps = 1e-05
masked_score = -1e30

MESH = pl.DeviceIdType.MESH

UNITS = ((0, 0), (1, 0), (3, 0), (0, 1), (1, 1), (3, 1), (2, 0), (2, 1))
ITEMS = ((0, 0, 2), (0, 2, 2)) + tuple((u, 0, 4) for u in range(1, 8))
PAIR_FIRST = frozenset((0, 2, 4, 5, 7))


def event_order():
    per_slot, hop = 0.87, 0.8
    entry = (0.7, 0.7, 5.0, 5.0, 5.5, 10.0, 11.0, 15.0, 18.0)
    links = ("pair", "up", "down")
    free = dict.fromkeys(links, 0.0)
    queue = {link: [] for link in links}
    count = itertools.count()
    events = [(entry[i], next(count), ("entry", i)) for i in range(len(ITEMS))]
    heapq.heapify(events)
    order = []
    while events:
        now, _, event = heapq.heappop(events)
        if event is not None:
            order.append(event)
            for link, arrival, slots in forwards(event):
                queue[link].append((arrival, slots))
        for link in links:
            if queue[link] and free[link] <= now + 1e-9:
                arrival, slots = queue[link].pop(0)
                free[link] = now + slots * per_slot
                heapq.heappush(events, (free[link] + hop, next(count), arrival))
                heapq.heappush(events, (free[link], next(count), None))
    return order


def forwards(event):
    kind, item = event[0], event[1]
    slots = ITEMS[item][2]
    sends = []
    if kind == "entry":
        sends += [("pair", ("pair", item), slots)]
        sends += [("up", ("up1", item, 0), slots), ("down", ("down1", item, 0), slots)]
    elif kind == "pair" and item in PAIR_FIRST:
        sends += [("up", ("up1", item, 1), slots), ("down", ("down1", item, 1), slots)]
    elif kind in ("up1", "down1"):
        link = kind[:-1]
        sends += [(link, (link + "2", item, event[2]), slots // 2)]
        if item not in PAIR_FIRST:
            sends += [("pair", ("late", item, kind), slots)]
    elif kind in ("up2", "down2") and item not in PAIR_FIRST:
        sends += [("pair", ("late", item, kind), slots // 2)]
    return sends


EVENTS = event_order()
PLACE = {event: i for i, event in enumerate(EVENTS)}
ARRIVALS = [event for event in EVENTS if event[0] != "entry"]
RECV = {event: i for i, event in enumerate(ARRIVALS)}
SPLIT = {event: i for i, event in enumerate(EVENTS[-8:])}
GROUP_ENDS = (14, 28, 42, 56, 68, 78, 84, 88, len(EVENTS))
GROUP = {event: sum(PLACE[event] >= end for end in GROUP_ENDS) for event in EVENTS}


def gather_kernel(
    hid_hbm,
    gain_hbm,
    buckets,
    slot_hbm,
    cache,
    freq_ref,
    len_hbm,
    arr,
    proj,
    cos_ref,
    sin_ref,
    kv,
    hid,
    gain,
    slot_row,
    inv_row,
    inv,
    len_ref,
    factor,
    turned,
    lhs,
    prep_sem,
    own_sem,
    recv_sem,
    split_sem,
    entry_sem,
    link_sem,
    stage_sem,
    kv_send,
    kv_recv,
    cache_send,
    cache_recv,
):
    r = lax.axis_index("replica")
    t = lax.axis_index("tensor")
    z, p = r // 2, r % 2
    x, h, c = t // 4, (t // 2) % 2, t % 2
    other_core = (r, x * 4 + h * 2 + (1 - c))
    next_replica = {
        "pair": z * 2 + (1 - p),
        "up": ((z + 1) % 4) * 2 + p,
        "down": ((z + 3) % 4) * 2 + p,
    }
    target = {link: (replica, t) for link, replica in next_replica.items()}
    across = {link: (replica, other_core[1]) for link, replica in next_replica.items()}
    own_col = pl.multiple_of(QC + HD * c, HD)
    other_col = pl.multiple_of(QC + HD * (1 - c), HD)

    prep = [
        pltpu.make_async_copy(hid_hbm, hid, prep_sem.at[0]),
        pltpu.make_async_copy(gain_hbm, gain, prep_sem.at[1]),
        pltpu.make_async_copy(slot_hbm, slot_row, prep_sem.at[2]),
        pltpu.make_async_copy(len_hbm, len_ref, prep_sem.at[3]),
    ]
    for copy in prep:
        copy.start()

    def chip(dx, dh, core):
        return (z * 2 + (p + dh) % 2, ((x + dx) % 4) * 4 + ((h + dh) % 2) * 2 + core)

    barrier = pltpu.get_barrier_semaphore()
    peers = [other_core] + list(target.values()) + list(across.values())
    peers += [chip(dx, dh, core) for dx, dh in UNITS[1:4] for core in range(2)]
    for peer in peers:
        pl.semaphore_signal(barrier, inc=1, device_id=peer, device_id_type=MESH)
    pl.semaphore_wait(barrier, len(peers))

    mine = (r * N_TENSOR + t) * 2
    sent = {"pair": 0, "up": 0, "down": 0}
    link_index = {"pair": 0, "up": 1, "down": 2}

    def parts(base, slots):
        rows = pl.ds(base, slots)
        return arr.at[rows, :, pl.ds(own_col, HD)], arr.at[rows, :, pl.ds(0, QC)]

    def bucket_parts(x_to, h_to, core):
        group = x_to * 2 + h_to
        query = pl.multiple_of((group * 2 + core) * QC, QC)
        key = pl.multiple_of(QH * HD + core * (KVH * HD) + group * HD, HD)
        return buckets.at[:, :, pl.ds(key, HD)], buckets.at[:, :, pl.ds(query, QC)]

    def own_columns(core):
        return pl.ds(pl.multiple_of(QC + HD * core, HD), HD), pl.ds(0, QC)

    def send_mine(x_to, h_to, core, dst, send_sem, recv_sems):
        for src, cols, recv in zip(bucket_parts(x_to, h_to, core), own_columns(core), recv_sems):
            pltpu.make_async_remote_copy(
                src_ref=src,
                dst_ref=arr.at[pl.ds(mine, 2), :, cols],
                send_sem=send_sem,
                recv_sem=recv,
                device_id=dst,
                device_id_type=MESH,
            ).start()

    def send_unit(unit):
        dx, dh = UNITS[unit]
        x_to, h_to, p_to = (x + 4 - dx) % 4, (h + dh) % 2, (p + dh) % 2
        sems = (entry_sem.at[unit], entry_sem.at[unit])
        for core in range(2):
            dst = (z * 2 + p_to, x_to * 4 + h_to * 2 + core)
            send_mine(x_to, h_to, core, dst, stage_sem.at[0], sems)

    def wait_bytes(slots, sem, width=OWN):
        ref = arr.at[pl.ds(0, slots), :, pl.ds(0, width)]
        pltpu.make_async_copy(ref, ref, sem).wait()

    def recv_of(event, part):
        if part == 0 and event in SPLIT:
            return split_sem.at[SPLIT[event]]
        return recv_sem.at[RECV[event]]

    for item, core in ((0, c), (1, 1 - c)):
        for link, arrival, slots in forwards(("entry", item)):
            dst = (target, across)[item][link]
            sems = (recv_of(arrival, 0), recv_of(arrival, 1))
            send_mine(x, h, core, dst, link_sem.at[link_index[link]], sems)
            sent[link] += slots
    own_copies = []
    for src, dst in zip(bucket_parts(x, h, c), parts(mine, 2)):
        copy = pltpu.make_async_copy(src, dst, own_sem.at[len(own_copies)])
        copy.start()
        own_copies.append(copy)
    send_mine(x, h, 1 - c, other_core, stage_sem.at[0], (entry_sem.at[0], entry_sem.at[0]))
    for unit in (1, 2, 3):
        send_unit(unit)

    def unit_base(unit, z_of, p_of):
        dx, dh = UNITS[unit]
        source = z_of * 2 + (p_of + dh) % 2
        return source * 32 + ((x + dx) % 4) * 8 + ((h + dh) % 2) * 4

    up_z, down_z, far_z = (z + 3) % 4, (z + 1) % 4, (z + 2) % 4

    def place(event):
        kind, item = event[0], event[1]
        unit, first, slots = ITEMS[item]
        if kind == "entry":
            z_of, p_of = z, p
        elif kind == "pair":
            z_of, p_of = z, 1 - p
        else:
            way = event[2] if kind == "late" else kind
            z_of = {"up1": up_z, "down1": down_z, "up2": far_z, "down2": far_z}[way]
            if kind == "late":
                p_of = 1 - p
            else:
                p_of = (p + event[2]) % 2
            if way in ("up2", "down2"):
                slots = slots // 2
                if way == "down2":
                    first = first + slots
        base = unit_base(unit, z_of, p_of)
        if unit == 0:
            own_half = 2 * c if item == 0 else 2 * (1 - c)
            base = base + own_half + (first - ITEMS[item][1])
        else:
            base = base + first
        return base, slots

    def wait_for(event, part):
        slots = place(event)[1]
        if event in SPLIT:
            wait_bytes(slots, recv_of(event, part), (HD, QC)[part])
        elif part == 0:
            return
        elif event == ("entry", 0):
            for copy in own_copies:
                copy.wait()
        elif event == ("entry", 1):
            wait_bytes(slots, entry_sem.at[0])
        elif event[0] == "entry":
            wait_bytes(slots, entry_sem.at[ITEMS[event[1]][0]])
        else:
            wait_bytes(slots, recv_of(event, 1))

    def forward(event, part):
        if event in (("entry", 0), ("entry", 1)):
            return
        base, _ = place(event)
        for link, arrival, slots in forwards(event):
            start = base
            if arrival[0] == "down2":
                start = base + slots
            ref = parts(start, slots)[part]
            pltpu.make_async_remote_copy(
                src_ref=ref,
                dst_ref=ref,
                send_sem=link_sem.at[link_index[link]],
                recv_sem=recv_of(arrival, part),
                device_id=target[link],
                device_id_type=MESH,
            ).start()
            if part == 1:
                sent[link] += slots

    def share(event):
        base, slots = place(event)
        ref = arr.at[pl.ds(base, slots), :, pl.ds(own_col, HD)]
        pltpu.make_async_remote_copy(
            src_ref=ref,
            dst_ref=ref,
            send_sem=kv_send.at[0],
            recv_sem=kv_recv.at[GROUP[event]],
            device_id=other_core,
            device_id_type=MESH,
        ).start()

    group_slots = [0] * len(GROUP_ENDS)
    for event in EVENTS:
        group_slots[GROUP[event]] += place(event)[1]

    def shared_wait(group):
        ref = arr.at[pl.ds(0, group_slots[group]), :, pl.ds(QC, HD)]
        pltpu.make_async_copy(ref, ref, kv_recv.at[group]).wait()

    own_half = pl.ds(pl.multiple_of(c * HALF, HALF), HALF)

    def send_cache(row):
        pltpu.make_async_copy(cache.at[row], kv.at[row, own_half], cache_send.at[1]).start()
        pltpu.make_async_remote_copy(
            src_ref=cache.at[row],
            dst_ref=kv.at[row, own_half],
            send_sem=cache_send.at[0],
            recv_sem=cache_recv.at[0],
            device_id=other_core,
            device_id_type=MESH,
        ).start()

    def squares(j, total):
        part = hid[:, pl.ds(pl.multiple_of(j * 512, 512), 512)].astype(jnp.float32)
        return total + jnp.sum(part * part, axis=-1, keepdims=True)

    def turn(j, carry):
        cols = pl.ds(pl.multiple_of(j * 128, 128), 128)
        part = hid[:, cols].astype(jnp.float32) * factor[...] * gain[:, cols]
        part = part.astype(jnp.bfloat16).astype(jnp.float32)
        part = jnp.transpose(part).astype(jnp.bfloat16)
        turned[pl.ds(j * 4, 4)] = part.reshape(4, BROWS, M)
        return carry

    def pick(j, carry):
        rows = [turned[inv[0, j * 4 + i]] for i in range(4)]
        part = jnp.concatenate(rows, axis=0).astype(jnp.float32)
        lhs[j] = jnp.transpose(part).astype(jnp.bfloat16)
        return carry

    move = pltpu.make_async_copy(inv_row, inv, prep_sem.at[4])

    def find_slots():
        for copy in prep:
            copy.wait()
        slots = jnp.broadcast_to(slot_row[...], (NB, NB))
        by_bucket = jnp.transpose(slots)
        hit = by_bucket == lax.broadcasted_iota(jnp.int32, (NB, NB), 1)
        bucket = lax.broadcasted_iota(jnp.int32, (NB, NB), 0)
        inv_row[...] = jnp.max(jnp.where(hit, bucket, 0), axis=0, keepdims=True)
        move.start()

    def find_factor():
        total = lax.fori_loop(0, D // 512, squares, jnp.zeros((M, 1), jnp.float32))
        factor[...] = jnp.broadcast_to(lax.rsqrt(total * (1.0 / D) + norm_eps), (M, HD))
        move.wait()

    def find_angles():
        row = lax.broadcasted_iota(jnp.int32, (M, HD), 0)
        position = jnp.zeros((M, HD), jnp.int32)
        for b in range(ROWS):
            for s in range(STEPS):
                position = jnp.where(row == s * ROWS + b, len_ref[b] + s, position)
        angle = position.astype(jnp.float32) * freq_ref[...]
        lane = lax.broadcasted_iota(jnp.int32, (M, HD), 1)
        cos_ref[...] = jnp.cos(angle)
        sine = jnp.sin(angle)
        sin_ref[...] = jnp.where(lane < HD // 2, -sine, sine)
        proj[...] = jnp.zeros_like(proj)

    slices = 8
    span = D // 128 // slices
    prepare = [find_slots, find_factor, find_angles]
    for body in (turn, pick):
        for i in range(slices):
            prepare.append(functools.partial(lax.fori_loop, i * span, (i + 1) * span, body, 0))
    prepare = iter(prepare)

    def multiply(base, column, width):
        rows = arr[pl.ds(base, 4), :, pl.ds(column, width)].reshape(4 * BROWS, width)
        return jnp.dot(lhs[base // 4], rows, preferred_element_type=jnp.float32)

    def add_own(base):
        base = pl.multiple_of(base, 4)
        proj[:, :QC] += multiply(base, 0, QC)
        proj[:, pl.ds(own_col, HD)] += multiply(base, own_col, HD)

    def add_other(base):
        base = pl.multiple_of(base, 4)
        proj[:, pl.ds(other_col, HD)] += multiply(base, other_col, HD)

    def unit_of(event):
        kind, item = event[0], event[1]
        unit = ITEMS[item][0]
        if kind in ("entry", "pair"):
            return (kind, unit)
        way = event[2] if kind == "late" else kind
        side = 1 if kind == "late" else event[2]
        far = way in ("up2", "down2")
        return ("far" if far else way, side, unit)

    missing = {}
    for event in EVENTS:
        missing.setdefault(unit_of(event), set()).add(event)
    base_of = {}
    ready = []
    for name, members in missing.items():
        some = next(event for event in EVENTS if event in members)
        kind = some[0]
        if kind == "entry":
            base_of[name] = unit_base(name[1], z, p)
        elif kind == "pair":
            base_of[name] = unit_base(name[1], z, 1 - p)
        else:
            z_of = {"up1": up_z, "down1": down_z, "far": far_z}[name[0]]
            base_of[name] = unit_base(name[2], z_of, (p + name[1]) % 2)
    members_of = {name: sorted(events, key=PLACE.get) for name, events in missing.items()}
    waiting_other = []
    shared = set()
    prepared = False
    cache_rows = iter(range(ROWS))
    for step, event in enumerate(EVENTS):
        if event in SPLIT:
            wait_for(event, 0)
            forward(event, 0)
            share(event)
            wait_for(event, 1)
            forward(event, 1)
        else:
            wait_for(event, 1)
            forward(event, 1)
            forward(event, 0)
            share(event)
        if event == ("entry", 4):
            for unit in (4, 5, 6):
                send_unit(unit)
        if event == ("entry", 5):
            send_unit(7)
        name = unit_of(event)
        missing[name].remove(event)
        if not missing[name]:
            ready.append(name)
        if step >= 20 and not prepared:
            work = next(prepare, None)
            if work is None:
                prepared = True
            else:
                work()
        if step >= 12:
            row = next(cache_rows, None)
            if row is not None:
                send_cache(row)
        if prepared:
            for name in ready[:2]:
                add_own(base_of[name])
                waiting_other.append(name)
            ready = ready[2:]
            for name in waiting_other[:2]:
                group = max(GROUP[member] for member in members_of[name])
                if step >= GROUP_ENDS[group] + 2:
                    for earlier in range(group + 1):
                        if earlier not in shared:
                            shared_wait(earlier)
                            shared.add(earlier)
                    add_other(base_of[name])
                    waiting_other.remove(name)
    for name in ready:
        add_own(base_of[name])
        waiting_other.append(name)
    for group in range(len(GROUP_ENDS)):
        if group not in shared:
            shared_wait(group)
    for name in waiting_other:
        add_other(base_of[name])

    for link, slots in sent.items():
        wait_bytes(slots, link_sem.at[link_index[link]])
    wait_bytes(30, stage_sem.at[0])
    everything = arr.at[:, :, pl.ds(QC, HD)]
    pltpu.make_async_copy(everything, everything, kv_send.at[0]).wait()
    pltpu.make_async_copy(cache, cache, cache_send.at[0]).wait()
    pltpu.make_async_copy(cache, cache, cache_send.at[1]).wait()
    pltpu.make_async_copy(cache, cache, cache_recv.at[0]).wait()


def attend_kernel(
    slot_ref,
    len_ref,
    arr,
    proj,
    cos_ref,
    sin_ref,
    kv,
    served,
    context,
    queries,
    scores,
    probs,
    outs,
    served_sem,
):
    def install(b):
        pltpu.make_async_copy(
            arr.at[slot_ref[b]], served.at[0, pl.ds(pl.multiple_of(b * BROWS, BROWS), BROWS)], served_sem.at[0]
        ).start()

    def install_all(b, carry):
        install(b)
        return carry

    lax.fori_loop(0, NB, install_all, 0, unroll=8)

    def rotate(block):
        return (block * cos_ref[...] + pltpu.roll(block, HD // 2, 1) * sin_ref[...]).astype(jnp.bfloat16)

    for head in range(HEADS):
        turned = rotate(proj[:, pl.ds(head * HD, HD)]).astype(jnp.float32)
        for s in range(STEPS):
            queries[:, s * HEADS + head, :] = turned[s * ROWS : (s + 1) * ROWS]
    keys_new = rotate(proj[:, pl.ds(QC, HD)]).astype(jnp.float32).reshape(STEPS, ROWS, 1, HD)
    values_new = proj[:, pl.ds(QC + HD, HD)].astype(jnp.bfloat16).astype(jnp.float32)
    values_new = values_new.reshape(STEPS, ROWS, 1, HD)

    scale_factor = HD ** (-0.5)
    position = lax.broadcasted_iota(jnp.int32, (1, LEN), 1)
    dims = (((1,), (1,)), ((), ()))

    def score(b, carry):
        found = lax.dot_general(
            queries[b].astype(jnp.bfloat16), kv[b, :, :HD], dims, preferred_element_type=jnp.float32
        )
        scores[b] = jnp.where(position < len_ref[b], found * scale_factor, masked_score)
        return carry

    lax.fori_loop(0, ROWS, score, 0, unroll=8)

    query = queries[...]
    fresh = [jnp.sum(query * keys_new[s], axis=-1, keepdims=True) * scale_factor for s in range(STEPS)]
    step = lax.broadcasted_iota(jnp.int32, (ROWS, STEPS * HEADS, 1), 1) // HEADS
    fresh[1] = jnp.where(step >= 1, fresh[1], masked_score)
    found = scores[...]
    peaks = jnp.maximum(jnp.max(found, axis=-1, keepdims=True), jnp.maximum(fresh[0], fresh[1]))
    weights = jnp.exp(found - peaks).astype(jnp.bfloat16)
    probs[...] = weights
    total = jnp.sum(weights.astype(jnp.float32), axis=-1, keepdims=True)
    fresh = [jnp.exp(one - peaks).astype(jnp.bfloat16).astype(jnp.float32) for one in fresh]
    total = total + fresh[0] + fresh[1]
    extra = fresh[0] * values_new[0] + fresh[1] * values_new[1]

    def gather(b, carry):
        outs[b] = jnp.dot(probs[b], kv[b, :, HD:], preferred_element_type=jnp.float32)
        return carry

    lax.fori_loop(0, ROWS, gather, 0, unroll=16)
    outs[...] = (outs[...] + extra) / total
    for head in range(HEADS):
        for s in range(STEPS):
            context[pl.ds(s * ROWS, ROWS), pl.ds(head * HD, HD)] = outs[:, s * HEADS + head, :].astype(jnp.bfloat16)
    pltpu.make_async_copy(served, served, served_sem.at[0]).wait()


def on_device(hidden_in, norm_gain, qkv_buckets, bucket_slot, kv_cache, cache_len):
    any_space = pl.BlockSpec(memory_space=pl.ANY)
    vmem = pl.BlockSpec(memory_space=pltpu.VMEM)
    smem = pl.BlockSpec(memory_space=pltpu.SMEM)
    freqs = rope_base ** (-2.0 * jnp.arange(HD // 2, dtype=jnp.float32) / HD)
    freqs = jnp.concatenate([freqs, freqs]).reshape(1, HD)
    dma = pltpu.SemaphoreType.DMA
    in_hbm = functools.partial(pltpu.with_memory_space_constraint, memory_space=pltpu.HBM)
    in_vmem = functools.partial(pltpu.with_memory_space_constraint, memory_space=pltpu.VMEM)
    arr, proj, cosine, sine, kv = pl.pallas_call(
        gather_kernel,
        out_shape=[
            pltpu.VMEM((NB, BROWS, COLS), jnp.bfloat16),
            pltpu.VMEM((M, COLS), jnp.float32),
            pltpu.VMEM((M, HD), jnp.float32),
            pltpu.VMEM((M, HD), jnp.float32),
            pltpu.VMEM((ROWS, LEN, 2 * HD), jnp.bfloat16),
        ],
        in_specs=[any_space] * 5 + [vmem, any_space],
        out_specs=[vmem] * 5,
        scratch_shapes=[
            pltpu.VMEM((M, D), jnp.bfloat16),
            pltpu.VMEM((1, D), jnp.float32),
            pltpu.VMEM((1, NB), jnp.int32),
            pltpu.VMEM((1, NB), jnp.int32),
            pltpu.SMEM((1, NB), jnp.int32),
            pltpu.SMEM((ROWS,), jnp.int32),
            pltpu.VMEM((M, HD), jnp.float32),
            pltpu.VMEM((NB, BROWS, M), jnp.bfloat16),
            pltpu.VMEM((NB // 4, M, 4 * BROWS), jnp.bfloat16),
            dma((5,)),
            dma((2,)),
            dma((len(ARRIVALS),)),
            dma((len(SPLIT),)),
            dma((len(UNITS),)),
            dma((3,)),
            dma((1,)),
            dma((1,)),
            dma((len(GROUP_ENDS),)),
            dma((2,)),
            dma((1,)),
        ],
        compiler_params=pltpu.CompilerParams(
            collective_id=0, has_side_effects=True, vmem_limit_bytes=10 * 2**20
        ),
        name="gather_and_project",
    )(
        in_hbm(hidden_in.reshape(M, D)),
        in_hbm(norm_gain.reshape(1, D)),
        in_hbm(qkv_buckets),
        in_hbm(bucket_slot.reshape(1, NB)),
        in_hbm(kv_cache),
        freqs,
        in_hbm(cache_len),
    )
    served, context = pl.pallas_call(
        attend_kernel,
        out_shape=[
            pltpu.HBM((1, D, COLS), jnp.bfloat16),
            jax.ShapeDtypeStruct((M, QC), jnp.bfloat16),
        ],
        in_specs=[smem, smem] + [vmem] * 5,
        out_specs=[any_space, vmem],
        scratch_shapes=[
            pltpu.VMEM((ROWS, STEPS * HEADS, HD), jnp.float32),
            pltpu.VMEM((ROWS, STEPS * HEADS, LEN), jnp.float32),
            pltpu.VMEM((ROWS, STEPS * HEADS, LEN), jnp.bfloat16),
            pltpu.VMEM((ROWS, STEPS * HEADS, HD), jnp.float32),
            dma((1,)),
        ],
        compiler_params=pltpu.CompilerParams(vmem_limit_bytes=12 * 2**20),
        name="attend_and_install",
    )(in_hbm(bucket_slot), in_hbm(cache_len), in_vmem(arr), in_vmem(proj), in_vmem(cosine), in_vmem(sine), in_vmem(kv))
    return context.reshape(STEPS, ROWS, QC), served


def solution(mesh):
    in_specs = (
        P(None, "replica", None),
        P(),
        P(("replica", "tensor"), None, None),
        P(),
        P("replica", "tensor", None),
        P("replica"),
    )
    out_specs = (P(None, "replica", "tensor"), P("tensor", None, None))
    return jax.shard_map(
        on_device, mesh=mesh, in_specs=in_specs, out_specs=out_specs, check_vma=False
    )
```

```python
import functools
import heapq
import itertools

import jax
import jax.numpy as jnp
import numpy as np
from jax import lax
from jax.experimental import pallas as pl
from jax.experimental.pallas import tpu as pltpu
from jax.sharding import PartitionSpec as P

QH = 64
KVH = 8
HD = 128
D = 8192
LEN = 2048
STEPS = 2
BROWS = 32
NB = 256
N_TENSOR = 16
N_REPLICA = 8
ROWS = 16
M = STEPS * ROWS
QC = 512
OWN = QC + HD
COLS = QC + 2 * HD
HEADS = QC // HD
HALF = LEN // 2

rope_base = 500000.0
norm_eps = 1e-05
masked_score = -1e30

MESH = pl.DeviceIdType.MESH

UNITS = ((0, 0), (1, 0), (3, 0), (0, 1), (1, 1), (3, 1), (2, 0), (2, 1))
ITEMS = ((0, 0, 2), (0, 2, 2)) + tuple((u, 0, 4) for u in range(1, 8))
PAIR_FIRST = frozenset((0, 2, 3, 7, 8))


def event_order():
    per_slot, hop = 0.87, 2.0
    entry = (0.7, 0.7, 5.0, 5.0, 5.5, 10.0, 11.0, 15.0, 18.0)
    links = ("pair", "up", "down")
    free = dict.fromkeys(links, 0.0)
    queue = {link: [] for link in links}
    count = itertools.count()
    events = [(entry[i], next(count), ("entry", i)) for i in range(len(ITEMS))]
    heapq.heapify(events)
    order = []
    while events:
        now, _, event = heapq.heappop(events)
        if event is not None:
            order.append(event)
            for link, arrival, slots in forwards(event):
                queue[link].append((arrival, slots))
        for link in links:
            if queue[link] and free[link] <= now + 1e-9:
                arrival, slots = queue[link].pop(0)
                free[link] = now + slots * per_slot
                heapq.heappush(events, (free[link] + hop, next(count), arrival))
                heapq.heappush(events, (free[link], next(count), None))
    return order


def forwards(event):
    kind, item = event[0], event[1]
    slots = ITEMS[item][2]
    sends = []
    if kind == "entry":
        sends += [("pair", ("pair", item), slots)]
        sends += [("up", ("up1", item, 0), slots), ("down", ("down1", item, 0), slots)]
    elif kind == "pair" and item in PAIR_FIRST:
        sends += [("up", ("up1", item, 1), slots), ("down", ("down1", item, 1), slots)]
    elif kind in ("up1", "down1"):
        link = kind[:-1]
        sends += [(link, (link + "2", item, event[2]), slots // 2)]
        if item not in PAIR_FIRST:
            sends += [("pair", ("late", item, kind), slots)]
    elif kind in ("up2", "down2") and item not in PAIR_FIRST:
        sends += [("pair", ("late", item, kind), slots // 2)]
    return sends


EVENTS = event_order()
PLACE = {event: i for i, event in enumerate(EVENTS)}
ARRIVALS = [event for event in EVENTS if event[0] != "entry"]
RECV = {event: i for i, event in enumerate(ARRIVALS)}
DIRECT = {event: i for i, event in enumerate(EVENTS[-3:])}
GROUP_ENDS = (14, 28, 42, 56, 68, 78, 82, 85, len(EVENTS) - len(DIRECT))
GROUP = {event: sum(PLACE[event] >= end for end in GROUP_ENDS) for event in EVENTS}


def gather_kernel(
    hid_hbm,
    gain_hbm,
    buckets,
    slot_hbm,
    cache,
    freq_ref,
    len_hbm,
    arr,
    proj,
    cos_ref,
    sin_ref,
    kv,
    hid,
    gain,
    slot_row,
    inv_row,
    inv,
    len_ref,
    factor,
    turned,
    lhs,
    prep_sem,
    own_sem,
    recv_sem,
    direct_send,
    direct_recv,
    entry_sem,
    link_sem,
    stage_sem,
    kv_send,
    kv_recv,
    cache_send,
    cache_recv,
):
    r = lax.axis_index("replica")
    t = lax.axis_index("tensor")
    z, p = r // 2, r % 2
    x, h, c = t // 4, (t // 2) % 2, t % 2
    other_core = (r, x * 4 + h * 2 + (1 - c))
    next_replica = {
        "pair": z * 2 + (1 - p),
        "up": ((z + 1) % 4) * 2 + p,
        "down": ((z + 3) % 4) * 2 + p,
    }
    target = {link: (replica, t) for link, replica in next_replica.items()}
    across = {link: (replica, other_core[1]) for link, replica in next_replica.items()}
    own_col = pl.multiple_of(QC + HD * c, HD)
    other_col = pl.multiple_of(QC + HD * (1 - c), HD)

    prep = [
        pltpu.make_async_copy(hid_hbm, hid, prep_sem.at[0]),
        pltpu.make_async_copy(gain_hbm, gain, prep_sem.at[1]),
        pltpu.make_async_copy(slot_hbm, slot_row, prep_sem.at[2]),
        pltpu.make_async_copy(len_hbm, len_ref, prep_sem.at[3]),
    ]
    for copy in prep:
        copy.start()

    def chip(dx, dh, core):
        return (z * 2 + (p + dh) % 2, ((x + dx) % 4) * 4 + ((h + dh) % 2) * 2 + core)

    barrier = pltpu.get_barrier_semaphore()
    peers = [other_core] + list(target.values()) + list(across.values())
    peers += [chip(dx, dh, core) for dx, dh in UNITS[1:4] for core in range(2)]
    for peer in peers:
        pl.semaphore_signal(barrier, inc=1, device_id=peer, device_id_type=MESH)
    pl.semaphore_wait(barrier, len(peers))

    mine = (r * N_TENSOR + t) * 2
    sent = {"pair": 0, "up": 0, "down": 0}
    link_index = {"pair": 0, "up": 1, "down": 2}

    def parts(base, slots):
        rows = pl.ds(base, slots)
        return arr.at[rows, :, pl.ds(own_col, HD)], arr.at[rows, :, pl.ds(0, QC)]

    def bucket_parts(x_to, h_to, core):
        group = x_to * 2 + h_to
        query = pl.multiple_of((group * 2 + core) * QC, QC)
        key = pl.multiple_of(QH * HD + core * (KVH * HD) + group * HD, HD)
        return buckets.at[:, :, pl.ds(key, HD)], buckets.at[:, :, pl.ds(query, QC)]

    def own_columns(core):
        return pl.ds(pl.multiple_of(QC + HD * core, HD), HD), pl.ds(0, QC)

    def send_mine(x_to, h_to, core, dst, send_sem, recv_sems):
        for src, cols, recv in zip(bucket_parts(x_to, h_to, core), own_columns(core), recv_sems):
            pltpu.make_async_remote_copy(
                src_ref=src,
                dst_ref=arr.at[pl.ds(mine, 2), :, cols],
                send_sem=send_sem,
                recv_sem=recv,
                device_id=dst,
                device_id_type=MESH,
            ).start()

    def send_unit(unit):
        dx, dh = UNITS[unit]
        x_to, h_to, p_to = (x + 4 - dx) % 4, (h + dh) % 2, (p + dh) % 2
        sems = (entry_sem.at[unit], entry_sem.at[unit])
        for core in range(2):
            dst = (z * 2 + p_to, x_to * 4 + h_to * 2 + core)
            send_mine(x_to, h_to, core, dst, stage_sem.at[0], sems)

    def wait_bytes(slots, sem, width=OWN):
        ref = arr.at[pl.ds(0, slots), :, pl.ds(0, width)]
        pltpu.make_async_copy(ref, ref, sem).wait()

    def recv_of(event):
        return recv_sem.at[RECV[event]]

    for item, core in ((0, c), (1, 1 - c)):
        for link, arrival, slots in forwards(("entry", item)):
            dst = (target, across)[item][link]
            sems = (recv_of(arrival), recv_of(arrival))
            send_mine(x, h, core, dst, link_sem.at[link_index[link]], sems)
            sent[link] += slots
    own_copies = []
    for src, dst in zip(bucket_parts(x, h, c), parts(mine, 2)):
        copy = pltpu.make_async_copy(src, dst, own_sem.at[len(own_copies)])
        copy.start()
        own_copies.append(copy)
    send_mine(x, h, 1 - c, other_core, stage_sem.at[0], (entry_sem.at[0], entry_sem.at[0]))
    for unit in (1, 2, 3):
        send_unit(unit)

    def unit_base(unit, z_of, p_of):
        dx, dh = UNITS[unit]
        source = z_of * 2 + (p_of + dh) % 2
        return source * 32 + ((x + dx) % 4) * 8 + ((h + dh) % 2) * 4

    up_z, down_z, far_z = (z + 3) % 4, (z + 1) % 4, (z + 2) % 4

    def place(event):
        kind, item = event[0], event[1]
        unit, first, slots = ITEMS[item]
        if kind == "entry":
            z_of, p_of = z, p
        elif kind == "pair":
            z_of, p_of = z, 1 - p
        else:
            way = event[2] if kind == "late" else kind
            z_of = {"up1": up_z, "down1": down_z, "up2": far_z, "down2": far_z}[way]
            if kind == "late":
                p_of = 1 - p
            else:
                p_of = (p + event[2]) % 2
            if way in ("up2", "down2"):
                slots = slots // 2
                if way == "down2":
                    first = first + slots
        base = unit_base(unit, z_of, p_of)
        if unit == 0:
            own_half = 2 * c if item == 0 else 2 * (1 - c)
            base = base + own_half + (first - ITEMS[item][1])
        else:
            base = base + first
        return base, slots

    def wait_for(event):
        slots = place(event)[1]
        if event == ("entry", 0):
            for copy in own_copies:
                copy.wait()
        elif event == ("entry", 1):
            wait_bytes(slots, entry_sem.at[0])
        elif event[0] == "entry":
            wait_bytes(slots, entry_sem.at[ITEMS[event[1]][0]])
        else:
            wait_bytes(slots, recv_of(event))

    def forward(event):
        if event in (("entry", 0), ("entry", 1)):
            return
        base, _ = place(event)
        for link, arrival, slots in forwards(event):
            start = base
            if arrival[0] == "down2":
                start = base + slots
            sends = [(ref, target[link], link_sem.at[link_index[link]], recv_of(arrival)) for ref in parts(start, slots)]
            if arrival in DIRECT:
                sends.insert(0, (sends[0][0], across[link], direct_send.at[0], direct_recv.at[DIRECT[arrival]]))
            for ref, dst, send_sem, recv in sends:
                pltpu.make_async_remote_copy(
                    src_ref=ref,
                    dst_ref=ref,
                    send_sem=send_sem,
                    recv_sem=recv,
                    device_id=dst,
                    device_id_type=MESH,
                ).start()
            sent[link] += slots

    def share(event):
        base, slots = place(event)
        ref = arr.at[pl.ds(base, slots), :, pl.ds(own_col, HD)]
        pltpu.make_async_remote_copy(
            src_ref=ref,
            dst_ref=ref,
            send_sem=kv_send.at[0],
            recv_sem=kv_recv.at[GROUP[event]],
            device_id=other_core,
            device_id_type=MESH,
        ).start()

    group_slots = [0] * len(GROUP_ENDS)
    for event in EVENTS:
        if event not in DIRECT:
            group_slots[GROUP[event]] += place(event)[1]
    direct_slots = [place(event)[1] for event in DIRECT]

    def shared_wait(group):
        ref = arr.at[pl.ds(0, group_slots[group]), :, pl.ds(QC, HD)]
        pltpu.make_async_copy(ref, ref, kv_recv.at[group]).wait()

    own_half = pl.ds(pl.multiple_of(c * HALF, HALF), HALF)

    def send_cache(row):
        pltpu.make_async_copy(cache.at[row], kv.at[row, own_half], cache_send.at[1]).start()
        pltpu.make_async_remote_copy(
            src_ref=cache.at[row],
            dst_ref=kv.at[row, own_half],
            send_sem=cache_send.at[0],
            recv_sem=cache_recv.at[0],
            device_id=other_core,
            device_id_type=MESH,
        ).start()

    def squares(j, total):
        part = hid[:, pl.ds(pl.multiple_of(j * 512, 512), 512)].astype(jnp.float32)
        return total + jnp.sum(part * part, axis=-1, keepdims=True)

    def turn(j, carry):
        cols = pl.ds(pl.multiple_of(j * 128, 128), 128)
        part = hid[:, cols].astype(jnp.float32) * factor[...] * gain[:, cols]
        part = part.astype(jnp.bfloat16).astype(jnp.float32)
        part = jnp.transpose(part).astype(jnp.bfloat16)
        turned[pl.ds(j * 4, 4)] = part.reshape(4, BROWS, M)
        return carry

    def pick(j, carry):
        rows = [turned[inv[0, j * 4 + i]] for i in range(4)]
        part = jnp.concatenate(rows, axis=0).astype(jnp.float32)
        lhs[j] = jnp.transpose(part).astype(jnp.bfloat16)
        return carry

    move = pltpu.make_async_copy(inv_row, inv, prep_sem.at[4])

    def find_slots():
        for copy in prep:
            copy.wait()
        slots = jnp.broadcast_to(slot_row[...], (NB, NB))
        by_bucket = jnp.transpose(slots)
        hit = by_bucket == lax.broadcasted_iota(jnp.int32, (NB, NB), 1)
        bucket = lax.broadcasted_iota(jnp.int32, (NB, NB), 0)
        inv_row[...] = jnp.max(jnp.where(hit, bucket, 0), axis=0, keepdims=True)
        move.start()

    def find_factor():
        total = lax.fori_loop(0, D // 512, squares, jnp.zeros((M, 1), jnp.float32))
        factor[...] = jnp.broadcast_to(lax.rsqrt(total * (1.0 / D) + norm_eps), (M, HD))
        move.wait()

    def find_angles():
        row = lax.broadcasted_iota(jnp.int32, (M, HD), 0)
        position = jnp.zeros((M, HD), jnp.int32)
        for b in range(ROWS):
            for s in range(STEPS):
                position = jnp.where(row == s * ROWS + b, len_ref[b] + s, position)
        angle = position.astype(jnp.float32) * freq_ref[...]
        lane = lax.broadcasted_iota(jnp.int32, (M, HD), 1)
        cos_ref[...] = jnp.cos(angle)
        sine = jnp.sin(angle)
        sin_ref[...] = jnp.where(lane < HD // 2, -sine, sine)
        proj[...] = jnp.zeros_like(proj)

    slices = 8
    span = D // 128 // slices
    prepare = [find_slots, find_factor, find_angles]
    for body in (turn, pick):
        for i in range(slices):
            prepare.append(functools.partial(lax.fori_loop, i * span, (i + 1) * span, body, 0))
    prepare = iter(prepare)

    def multiply(base, column, width):
        rows = arr[pl.ds(base, 4), :, pl.ds(column, width)].reshape(4 * BROWS, width)
        return jnp.dot(lhs[base // 4], rows, preferred_element_type=jnp.float32)

    def add_own(base):
        base = pl.multiple_of(base, 4)
        proj[:, :QC] += multiply(base, 0, QC)
        proj[:, pl.ds(own_col, HD)] += multiply(base, own_col, HD)

    def add_other(base):
        base = pl.multiple_of(base, 4)
        proj[:, pl.ds(other_col, HD)] += multiply(base, other_col, HD)

    def unit_of(event):
        kind, item = event[0], event[1]
        unit = ITEMS[item][0]
        if kind in ("entry", "pair"):
            return (kind, unit)
        way = event[2] if kind == "late" else kind
        side = 1 if kind == "late" else event[2]
        far = way in ("up2", "down2")
        return ("far" if far else way, side, unit)

    missing = {}
    for event in EVENTS:
        missing.setdefault(unit_of(event), set()).add(event)
    base_of = {}
    ready = []
    for name, members in missing.items():
        some = next(event for event in EVENTS if event in members)
        kind = some[0]
        if kind == "entry":
            base_of[name] = unit_base(name[1], z, p)
        elif kind == "pair":
            base_of[name] = unit_base(name[1], z, 1 - p)
        else:
            z_of = {"up1": up_z, "down1": down_z, "far": far_z}[name[0]]
            base_of[name] = unit_base(name[2], z_of, (p + name[1]) % 2)
    members_of = {name: sorted(events, key=PLACE.get) for name, events in missing.items()}
    waiting_other = []
    shared = set()
    prepared = False
    cache_rows = iter(range(ROWS))
    for step, event in enumerate(EVENTS):
        wait_for(event)
        forward(event)
        if event not in DIRECT:
            share(event)
        if event == ("entry", 4):
            for unit in (4, 5, 6):
                send_unit(unit)
        if event == ("entry", 5):
            send_unit(7)
        name = unit_of(event)
        missing[name].remove(event)
        if not missing[name]:
            ready.append(name)
        if step >= 20 and not prepared:
            work = next(prepare, None)
            if work is None:
                prepared = True
            else:
                work()
        if step >= 12:
            row = next(cache_rows, None)
            if row is not None:
                send_cache(row)
        if prepared:
            for name in ready[:2]:
                add_own(base_of[name])
                waiting_other.append(name)
            ready = ready[2:]
            for name in waiting_other[:2]:
                group = max(GROUP[member] for member in members_of[name])
                if group < len(GROUP_ENDS) and step >= GROUP_ENDS[group] + 2:
                    for earlier in range(group + 1):
                        if earlier not in shared:
                            shared_wait(earlier)
                            shared.add(earlier)
                    add_other(base_of[name])
                    waiting_other.remove(name)
    for name in ready:
        add_own(base_of[name])
        waiting_other.append(name)
    for group in range(len(GROUP_ENDS)):
        if group not in shared:
            shared_wait(group)
    for i, slots in enumerate(direct_slots):
        wait_bytes(slots, direct_recv.at[i], HD)
    for name in waiting_other:
        add_other(base_of[name])

    for link, slots in sent.items():
        wait_bytes(slots, link_sem.at[link_index[link]])
    wait_bytes(30, stage_sem.at[0])
    wait_bytes(sum(group_slots), kv_send.at[0], HD)
    wait_bytes(sum(direct_slots), direct_send.at[0], HD)
    pltpu.make_async_copy(cache, cache, cache_send.at[0]).wait()
    pltpu.make_async_copy(cache, cache, cache_send.at[1]).wait()
    pltpu.make_async_copy(cache, cache, cache_recv.at[0]).wait()


def attend_kernel(
    slot_ref,
    len_ref,
    arr,
    proj,
    cos_ref,
    sin_ref,
    kv,
    served,
    context,
    queries,
    scores,
    probs,
    outs,
    served_sem,
):
    def install(b):
        pltpu.make_async_copy(
            arr.at[slot_ref[b]], served.at[0, pl.ds(pl.multiple_of(b * BROWS, BROWS), BROWS)], served_sem.at[0]
        ).start()

    def install_all(b, carry):
        install(b)
        return carry

    lax.fori_loop(0, NB, install_all, 0, unroll=8)

    def rotate(block):
        return (block * cos_ref[...] + pltpu.roll(block, HD // 2, 1) * sin_ref[...]).astype(jnp.bfloat16)

    for head in range(HEADS):
        turned = rotate(proj[:, pl.ds(head * HD, HD)]).astype(jnp.float32)
        for s in range(STEPS):
            queries[:, s * HEADS + head, :] = turned[s * ROWS : (s + 1) * ROWS]
    keys_new = rotate(proj[:, pl.ds(QC, HD)]).astype(jnp.float32).reshape(STEPS, ROWS, 1, HD)
    values_new = proj[:, pl.ds(QC + HD, HD)].astype(jnp.bfloat16).astype(jnp.float32)
    values_new = values_new.reshape(STEPS, ROWS, 1, HD)

    scale_factor = HD ** (-0.5)
    position = lax.broadcasted_iota(jnp.int32, (1, LEN), 1)
    dims = (((1,), (1,)), ((), ()))

    def score(b, carry):
        found = lax.dot_general(
            queries[b].astype(jnp.bfloat16), kv[b, :, :HD], dims, preferred_element_type=jnp.float32
        )
        scores[b] = jnp.where(position < len_ref[b], found * scale_factor, masked_score)
        return carry

    lax.fori_loop(0, ROWS, score, 0, unroll=8)

    query = queries[...]
    fresh = [jnp.sum(query * keys_new[s], axis=-1, keepdims=True) * scale_factor for s in range(STEPS)]
    step = lax.broadcasted_iota(jnp.int32, (ROWS, STEPS * HEADS, 1), 1) // HEADS
    fresh[1] = jnp.where(step >= 1, fresh[1], masked_score)
    found = scores[...]
    peaks = jnp.maximum(jnp.max(found, axis=-1, keepdims=True), jnp.maximum(fresh[0], fresh[1]))
    weights = jnp.exp(found - peaks).astype(jnp.bfloat16)
    probs[...] = weights
    total = jnp.sum(weights.astype(jnp.float32), axis=-1, keepdims=True)
    fresh = [jnp.exp(one - peaks).astype(jnp.bfloat16).astype(jnp.float32) for one in fresh]
    total = total + fresh[0] + fresh[1]
    extra = fresh[0] * values_new[0] + fresh[1] * values_new[1]

    def gather(b, carry):
        outs[b] = jnp.dot(probs[b], kv[b, :, HD:], preferred_element_type=jnp.float32)
        return carry

    lax.fori_loop(0, ROWS, gather, 0, unroll=16)
    outs[...] = (outs[...] + extra) / total
    for head in range(HEADS):
        for s in range(STEPS):
            context[pl.ds(s * ROWS, ROWS), pl.ds(head * HD, HD)] = outs[:, s * HEADS + head, :].astype(jnp.bfloat16)
    pltpu.make_async_copy(served, served, served_sem.at[0]).wait()


def on_device(hidden_in, norm_gain, qkv_buckets, bucket_slot, kv_cache, cache_len):
    any_space = pl.BlockSpec(memory_space=pl.ANY)
    vmem = pl.BlockSpec(memory_space=pltpu.VMEM)
    smem = pl.BlockSpec(memory_space=pltpu.SMEM)
    freqs = rope_base ** (-2.0 * jnp.arange(HD // 2, dtype=jnp.float32) / HD)
    freqs = jnp.concatenate([freqs, freqs]).reshape(1, HD)
    dma = pltpu.SemaphoreType.DMA
    in_hbm = functools.partial(pltpu.with_memory_space_constraint, memory_space=pltpu.HBM)
    in_vmem = functools.partial(pltpu.with_memory_space_constraint, memory_space=pltpu.VMEM)
    arr, proj, cosine, sine, kv = pl.pallas_call(
        gather_kernel,
        out_shape=[
            pltpu.VMEM((NB, BROWS, COLS), jnp.bfloat16),
            pltpu.VMEM((M, COLS), jnp.float32),
            pltpu.VMEM((M, HD), jnp.float32),
            pltpu.VMEM((M, HD), jnp.float32),
            pltpu.VMEM((ROWS, LEN, 2 * HD), jnp.bfloat16),
        ],
        in_specs=[any_space] * 5 + [vmem, any_space],
        out_specs=[vmem] * 5,
        scratch_shapes=[
            pltpu.VMEM((M, D), jnp.bfloat16),
            pltpu.VMEM((1, D), jnp.float32),
            pltpu.VMEM((1, NB), jnp.int32),
            pltpu.VMEM((1, NB), jnp.int32),
            pltpu.SMEM((1, NB), jnp.int32),
            pltpu.SMEM((ROWS,), jnp.int32),
            pltpu.VMEM((M, HD), jnp.float32),
            pltpu.VMEM((NB, BROWS, M), jnp.bfloat16),
            pltpu.VMEM((NB // 4, M, 4 * BROWS), jnp.bfloat16),
            dma((5,)),
            dma((2,)),
            dma((len(ARRIVALS),)),
            dma((1,)),
            dma((len(DIRECT),)),
            dma((len(UNITS),)),
            dma((3,)),
            dma((1,)),
            dma((1,)),
            dma((len(GROUP_ENDS),)),
            dma((2,)),
            dma((1,)),
        ],
        compiler_params=pltpu.CompilerParams(
            collective_id=0, has_side_effects=True, vmem_limit_bytes=10 * 2**20
        ),
        name="gather_and_project",
    )(
        in_hbm(hidden_in.reshape(M, D)),
        in_hbm(norm_gain.reshape(1, D)),
        in_hbm(qkv_buckets),
        in_hbm(bucket_slot.reshape(1, NB)),
        in_hbm(kv_cache),
        freqs,
        in_hbm(cache_len),
    )
    served, context = pl.pallas_call(
        attend_kernel,
        out_shape=[
            pltpu.HBM((1, D, COLS), jnp.bfloat16),
            jax.ShapeDtypeStruct((M, QC), jnp.bfloat16),
        ],
        in_specs=[smem, smem] + [vmem] * 5,
        out_specs=[any_space, vmem],
        scratch_shapes=[
            pltpu.VMEM((ROWS, STEPS * HEADS, HD), jnp.float32),
            pltpu.VMEM((ROWS, STEPS * HEADS, LEN), jnp.float32),
            pltpu.VMEM((ROWS, STEPS * HEADS, LEN), jnp.bfloat16),
            pltpu.VMEM((ROWS, STEPS * HEADS, HD), jnp.float32),
            dma((1,)),
        ],
        compiler_params=pltpu.CompilerParams(vmem_limit_bytes=12 * 2**20),
        name="attend_and_install",
    )(in_hbm(bucket_slot), in_hbm(cache_len), in_vmem(arr), in_vmem(proj), in_vmem(cosine), in_vmem(sine), in_vmem(kv))
    return context.reshape(STEPS, ROWS, QC), served


def solution(mesh):
    in_specs = (
        P(None, "replica", None),
        P(),
        P(("replica", "tensor"), None, None),
        P(),
        P("replica", "tensor", None),
        P("replica"),
    )
    out_specs = (P(None, "replica", "tensor"), P("tensor", None, None))
    return jax.shard_map(
        on_device, mesh=mesh, in_specs=in_specs, out_specs=out_specs, check_vma=False
    )
```

```python
import functools
import heapq
import itertools

import jax
import jax.numpy as jnp
import numpy as np
from jax import lax
from jax.experimental import pallas as pl
from jax.experimental.pallas import tpu as pltpu
from jax.sharding import PartitionSpec as P

QH = 64
KVH = 8
HD = 128
D = 8192
LEN = 2048
STEPS = 2
BROWS = 32
NB = 256
N_TENSOR = 16
N_REPLICA = 8
ROWS = 16
M = STEPS * ROWS
QC = 512
OWN = QC + HD
COLS = QC + 2 * HD
HEADS = QC // HD
HALF = LEN // 2

rope_base = 500000.0
norm_eps = 1e-05
masked_score = -1e30

MESH = pl.DeviceIdType.MESH

UNITS = ((0, 0), (1, 0), (3, 0), (0, 1), (1, 1), (3, 1), (2, 0), (2, 1))
ITEMS = ((0, 0, 2), (0, 2, 2)) + tuple((u, 0, 4) for u in range(1, 8))
PAIR_FIRST = frozenset((0, 2, 3, 7, 8))


def event_order():
    per_slot, hop = 0.87, 2.5
    entry = (0.7, 0.7, 5.0, 5.0, 5.5, 10.0, 11.0, 15.0, 18.0)
    links = ("pair", "up", "down")
    free = dict.fromkeys(links, 0.0)
    queue = {link: [] for link in links}
    count = itertools.count()
    events = [(entry[i], next(count), ("entry", i)) for i in range(len(ITEMS))]
    heapq.heapify(events)
    order = []
    while events:
        now, _, event = heapq.heappop(events)
        if event is not None:
            order.append(event)
            for link, arrival, slots in forwards(event):
                queue[link].append((arrival, slots))
        for link in links:
            if queue[link] and free[link] <= now + 1e-9:
                arrival, slots = queue[link].pop(0)
                free[link] = now + slots * per_slot
                heapq.heappush(events, (free[link] + hop, next(count), arrival))
                heapq.heappush(events, (free[link], next(count), None))
    return order


def forwards(event):
    kind, item = event[0], event[1]
    slots = ITEMS[item][2]
    sends = []
    if kind == "entry":
        sends += [("pair", ("pair", item), slots)]
        sends += [("up", ("up1", item, 0), slots), ("down", ("down1", item, 0), slots)]
    elif kind == "pair" and item in PAIR_FIRST:
        sends += [("up", ("up1", item, 1), slots), ("down", ("down1", item, 1), slots)]
    elif kind in ("up1", "down1"):
        link = kind[:-1]
        sends += [(link, (link + "2", item, event[2]), slots // 2)]
        if item not in PAIR_FIRST:
            sends += [("pair", ("late", item, kind), slots)]
    elif kind in ("up2", "down2") and item not in PAIR_FIRST:
        sends += [("pair", ("late", item, kind), slots // 2)]
    return sends


EVENTS = event_order()
PLACE = {event: i for i, event in enumerate(EVENTS)}
ARRIVALS = [event for event in EVENTS if event[0] != "entry"]
BOTH = {"up1": "round1", "down1": "round1", "up2": "round2", "down2": "round2"}
SHARED = list(dict.fromkeys((BOTH.get(event[0], event[0]),) + event[1:] for event in ARRIVALS))
RECV = {event: SHARED.index((BOTH.get(event[0], event[0]),) + event[1:]) for event in ARRIVALS}
DIRECT = {event: i for i, event in enumerate(EVENTS[-3:])}
GROUP_ENDS = (14, 28, 42, 56, 68, 78, 82, 85, len(EVENTS) - len(DIRECT))
GROUP = {event: sum(PLACE[event] >= end for end in GROUP_ENDS) for event in EVENTS}


def gather_kernel(
    hid_hbm,
    gain_hbm,
    buckets,
    slot_hbm,
    cache,
    freq_ref,
    len_hbm,
    arr,
    proj,
    cos_ref,
    sin_ref,
    kv,
    hid,
    gain,
    slot_row,
    inv_row,
    inv,
    len_ref,
    factor,
    turned,
    lhs,
    prep_sem,
    own_sem,
    recv_sem,
    direct_send,
    direct_recv,
    entry_sem,
    link_sem,
    stage_sem,
    kv_send,
    kv_recv,
    cache_send,
    cache_recv,
):
    r = lax.axis_index("replica")
    t = lax.axis_index("tensor")
    z, p = r // 2, r % 2
    x, h, c = t // 4, (t // 2) % 2, t % 2
    other_core = (r, x * 4 + h * 2 + (1 - c))
    next_replica = {
        "pair": z * 2 + (1 - p),
        "up": ((z + 1) % 4) * 2 + p,
        "down": ((z + 3) % 4) * 2 + p,
    }
    target = {link: (replica, t) for link, replica in next_replica.items()}
    across = {link: (replica, other_core[1]) for link, replica in next_replica.items()}
    own_col = pl.multiple_of(QC + HD * c, HD)
    other_col = pl.multiple_of(QC + HD * (1 - c), HD)

    prep = [
        pltpu.make_async_copy(hid_hbm, hid, prep_sem.at[0]),
        pltpu.make_async_copy(gain_hbm, gain, prep_sem.at[1]),
        pltpu.make_async_copy(slot_hbm, slot_row, prep_sem.at[2]),
        pltpu.make_async_copy(len_hbm, len_ref, prep_sem.at[3]),
    ]
    for copy in prep:
        copy.start()

    def chip(dx, dh, core):
        return (z * 2 + (p + dh) % 2, ((x + dx) % 4) * 4 + ((h + dh) % 2) * 2 + core)

    barrier = pltpu.get_barrier_semaphore()
    peers = [other_core] + list(target.values()) + list(across.values())
    peers += [chip(dx, dh, core) for dx, dh in UNITS[1:4] for core in range(2)]
    for peer in peers:
        pl.semaphore_signal(barrier, inc=1, device_id=peer, device_id_type=MESH)
    pl.semaphore_wait(barrier, len(peers))

    mine = (r * N_TENSOR + t) * 2
    sent = {"pair": 0, "up": 0, "down": 0}
    link_index = {"pair": 0, "up": 1, "down": 2}

    def parts(base, slots):
        rows = pl.ds(base, slots)
        return arr.at[rows, :, pl.ds(own_col, HD)], arr.at[rows, :, pl.ds(0, QC)]

    def bucket_parts(x_to, h_to, core):
        group = x_to * 2 + h_to
        query = pl.multiple_of((group * 2 + core) * QC, QC)
        key = pl.multiple_of(QH * HD + core * (KVH * HD) + group * HD, HD)
        return buckets.at[:, :, pl.ds(key, HD)], buckets.at[:, :, pl.ds(query, QC)]

    def own_columns(core):
        return pl.ds(pl.multiple_of(QC + HD * core, HD), HD), pl.ds(0, QC)

    def send_mine(x_to, h_to, core, dst, send_sem, recv_sems):
        for src, cols, recv in zip(bucket_parts(x_to, h_to, core), own_columns(core), recv_sems):
            pltpu.make_async_remote_copy(
                src_ref=src,
                dst_ref=arr.at[pl.ds(mine, 2), :, cols],
                send_sem=send_sem,
                recv_sem=recv,
                device_id=dst,
                device_id_type=MESH,
            ).start()

    def send_unit(unit):
        dx, dh = UNITS[unit]
        x_to, h_to, p_to = (x + 4 - dx) % 4, (h + dh) % 2, (p + dh) % 2
        sems = (entry_sem.at[unit], entry_sem.at[unit])
        for core in range(2):
            dst = (z * 2 + p_to, x_to * 4 + h_to * 2 + core)
            send_mine(x_to, h_to, core, dst, stage_sem.at[0], sems)

    def wait_bytes(slots, sem, width=OWN):
        ref = arr.at[pl.ds(0, slots), :, pl.ds(0, width)]
        pltpu.make_async_copy(ref, ref, sem).wait()

    def recv_of(event):
        return recv_sem.at[RECV[event]]

    for item, core in ((0, c), (1, 1 - c)):
        for link, arrival, slots in forwards(("entry", item)):
            dst = (target, across)[item][link]
            sems = (recv_of(arrival), recv_of(arrival))
            send_mine(x, h, core, dst, link_sem.at[link_index[link]], sems)
            sent[link] += slots
    own_copies = []
    for src, dst in zip(bucket_parts(x, h, c), parts(mine, 2)):
        copy = pltpu.make_async_copy(src, dst, own_sem.at[len(own_copies)])
        copy.start()
        own_copies.append(copy)
    send_mine(x, h, 1 - c, other_core, stage_sem.at[0], (entry_sem.at[0], entry_sem.at[0]))
    for unit in (1, 2, 3):
        send_unit(unit)

    def unit_base(unit, z_of, p_of):
        dx, dh = UNITS[unit]
        source = z_of * 2 + (p_of + dh) % 2
        return source * 32 + ((x + dx) % 4) * 8 + ((h + dh) % 2) * 4

    up_z, down_z, far_z = (z + 3) % 4, (z + 1) % 4, (z + 2) % 4

    def place(event):
        kind, item = event[0], event[1]
        unit, first, slots = ITEMS[item]
        if kind == "entry":
            z_of, p_of = z, p
        elif kind == "pair":
            z_of, p_of = z, 1 - p
        else:
            way = event[2] if kind == "late" else kind
            z_of = {"up1": up_z, "down1": down_z, "up2": far_z, "down2": far_z}[way]
            if kind == "late":
                p_of = 1 - p
            else:
                p_of = (p + event[2]) % 2
            if way in ("up2", "down2"):
                slots = slots // 2
                if way == "down2":
                    first = first + slots
        base = unit_base(unit, z_of, p_of)
        if unit == 0:
            own_half = 2 * c if item == 0 else 2 * (1 - c)
            base = base + own_half + (first - ITEMS[item][1])
        else:
            base = base + first
        return base, slots

    waited = set()

    def wait_for(event):
        slots = place(event)[1]
        if event == ("entry", 0):
            for copy in own_copies:
                copy.wait()
        elif event == ("entry", 1):
            wait_bytes(slots, entry_sem.at[0])
        elif event[0] == "entry":
            wait_bytes(slots, entry_sem.at[ITEMS[event[1]][0]])
        elif event[0] not in BOTH:
            wait_bytes(slots, recv_of(event))
        elif RECV[event] not in waited:
            waited.add(RECV[event])
            wait_bytes(2 * slots, recv_of(event))

    def forward(event):
        if event in (("entry", 0), ("entry", 1)):
            return
        base, _ = place(event)
        for link, arrival, slots in forwards(event):
            start = base
            if arrival[0] == "down2":
                start = base + slots
            sends = [(ref, target[link], link_sem.at[link_index[link]], recv_of(arrival)) for ref in parts(start, slots)]
            if arrival in DIRECT:
                sends.insert(0, (sends[0][0], across[link], direct_send.at[0], direct_recv.at[DIRECT[arrival]]))
            for ref, dst, send_sem, recv in sends:
                pltpu.make_async_remote_copy(
                    src_ref=ref,
                    dst_ref=ref,
                    send_sem=send_sem,
                    recv_sem=recv,
                    device_id=dst,
                    device_id_type=MESH,
                ).start()
            sent[link] += slots

    def share(event):
        base, slots = place(event)
        ref = arr.at[pl.ds(base, slots), :, pl.ds(own_col, HD)]
        pltpu.make_async_remote_copy(
            src_ref=ref,
            dst_ref=ref,
            send_sem=kv_send.at[0],
            recv_sem=kv_recv.at[GROUP[event]],
            device_id=other_core,
            device_id_type=MESH,
        ).start()

    group_slots = [0] * len(GROUP_ENDS)
    for event in EVENTS:
        if event not in DIRECT:
            group_slots[GROUP[event]] += place(event)[1]
    direct_slots = [place(event)[1] for event in DIRECT]

    def shared_wait(group):
        ref = arr.at[pl.ds(0, group_slots[group]), :, pl.ds(QC, HD)]
        pltpu.make_async_copy(ref, ref, kv_recv.at[group]).wait()

    own_half = pl.ds(pl.multiple_of(c * HALF, HALF), HALF)

    def send_cache(row):
        pltpu.make_async_copy(cache.at[row], kv.at[row, own_half], cache_send.at[1]).start()
        pltpu.make_async_remote_copy(
            src_ref=cache.at[row],
            dst_ref=kv.at[row, own_half],
            send_sem=cache_send.at[0],
            recv_sem=cache_recv.at[0],
            device_id=other_core,
            device_id_type=MESH,
        ).start()

    def squares(j, total):
        part = hid[:, pl.ds(pl.multiple_of(j * 512, 512), 512)].astype(jnp.float32)
        return total + jnp.sum(part * part, axis=-1, keepdims=True)

    def turn(j, carry):
        cols = pl.ds(pl.multiple_of(j * 128, 128), 128)
        part = hid[:, cols].astype(jnp.float32) * factor[...] * gain[:, cols]
        part = part.astype(jnp.bfloat16).astype(jnp.float32)
        part = jnp.transpose(part).astype(jnp.bfloat16)
        turned[pl.ds(j * 4, 4)] = part.reshape(4, BROWS, M)
        return carry

    def pick(j, carry):
        rows = [turned[inv[0, j * 4 + i]] for i in range(4)]
        part = jnp.concatenate(rows, axis=0).astype(jnp.float32)
        lhs[j] = jnp.transpose(part).astype(jnp.bfloat16)
        return carry

    move = pltpu.make_async_copy(inv_row, inv, prep_sem.at[4])

    def find_slots():
        for copy in prep:
            copy.wait()
        slots = jnp.broadcast_to(slot_row[...], (NB, NB))
        by_bucket = jnp.transpose(slots)
        hit = by_bucket == lax.broadcasted_iota(jnp.int32, (NB, NB), 1)
        bucket = lax.broadcasted_iota(jnp.int32, (NB, NB), 0)
        inv_row[...] = jnp.max(jnp.where(hit, bucket, 0), axis=0, keepdims=True)
        move.start()

    def find_factor():
        total = lax.fori_loop(0, D // 512, squares, jnp.zeros((M, 1), jnp.float32))
        factor[...] = jnp.broadcast_to(lax.rsqrt(total * (1.0 / D) + norm_eps), (M, HD))
        move.wait()

    def find_angles():
        row = lax.broadcasted_iota(jnp.int32, (M, HD), 0)
        position = jnp.zeros((M, HD), jnp.int32)
        for b in range(ROWS):
            for s in range(STEPS):
                position = jnp.where(row == s * ROWS + b, len_ref[b] + s, position)
        angle = position.astype(jnp.float32) * freq_ref[...]
        lane = lax.broadcasted_iota(jnp.int32, (M, HD), 1)
        cos_ref[...] = jnp.cos(angle)
        sine = jnp.sin(angle)
        sin_ref[...] = jnp.where(lane < HD // 2, -sine, sine)
        proj[...] = jnp.zeros_like(proj)

    slices = 8
    span = D // 128 // slices
    prepare = [find_slots, find_factor, find_angles]
    for body in (turn, pick):
        for i in range(slices):
            prepare.append(functools.partial(lax.fori_loop, i * span, (i + 1) * span, body, 0))
    prepare = iter(prepare)

    def multiply(base, column, width):
        rows = arr[pl.ds(base, 4), :, pl.ds(column, width)].reshape(4 * BROWS, width)
        return jnp.dot(lhs[base // 4], rows, preferred_element_type=jnp.float32)

    def add_own(base):
        base = pl.multiple_of(base, 4)
        proj[:, :QC] += multiply(base, 0, QC)
        proj[:, pl.ds(own_col, HD)] += multiply(base, own_col, HD)

    def add_other(base):
        base = pl.multiple_of(base, 4)
        proj[:, pl.ds(other_col, HD)] += multiply(base, other_col, HD)

    def unit_of(event):
        kind, item = event[0], event[1]
        unit = ITEMS[item][0]
        if kind in ("entry", "pair"):
            return (kind, unit)
        way = event[2] if kind == "late" else kind
        side = 1 if kind == "late" else event[2]
        far = way in ("up2", "down2")
        return ("far" if far else way, side, unit)

    missing = {}
    for event in EVENTS:
        missing.setdefault(unit_of(event), set()).add(event)
    base_of = {}
    ready = []
    for name, members in missing.items():
        some = next(event for event in EVENTS if event in members)
        kind = some[0]
        if kind == "entry":
            base_of[name] = unit_base(name[1], z, p)
        elif kind == "pair":
            base_of[name] = unit_base(name[1], z, 1 - p)
        else:
            z_of = {"up1": up_z, "down1": down_z, "far": far_z}[name[0]]
            base_of[name] = unit_base(name[2], z_of, (p + name[1]) % 2)
    members_of = {name: sorted(events, key=PLACE.get) for name, events in missing.items()}
    waiting_other = []
    shared = set()
    prepared = False
    cache_rows = iter(range(ROWS))
    for step, event in enumerate(EVENTS):
        wait_for(event)
        forward(event)
        if event not in DIRECT:
            share(event)
        if event == ("entry", 4):
            for unit in (4, 5, 6):
                send_unit(unit)
        if event == ("entry", 5):
            send_unit(7)
        name = unit_of(event)
        missing[name].remove(event)
        if not missing[name]:
            ready.append(name)
        if step >= 20 and not prepared:
            work = next(prepare, None)
            if work is None:
                prepared = True
            else:
                work()
        if step >= 12:
            row = next(cache_rows, None)
            if row is not None:
                send_cache(row)
        if prepared:
            for name in ready[:2]:
                add_own(base_of[name])
                waiting_other.append(name)
            ready = ready[2:]
            for name in waiting_other[:2]:
                group = max(GROUP[member] for member in members_of[name])
                if group < len(GROUP_ENDS) and step >= GROUP_ENDS[group] + 2:
                    for earlier in range(group + 1):
                        if earlier not in shared:
                            shared_wait(earlier)
                            shared.add(earlier)
                    add_other(base_of[name])
                    waiting_other.remove(name)
    for name in ready:
        add_own(base_of[name])
        waiting_other.append(name)
    for group in range(len(GROUP_ENDS)):
        if group not in shared:
            shared_wait(group)
    for i, slots in enumerate(direct_slots):
        wait_bytes(slots, direct_recv.at[i], HD)
    for name in waiting_other:
        add_other(base_of[name])

    for link, slots in sent.items():
        wait_bytes(slots, link_sem.at[link_index[link]])
    wait_bytes(30, stage_sem.at[0])
    wait_bytes(sum(group_slots), kv_send.at[0], HD)
    wait_bytes(sum(direct_slots), direct_send.at[0], HD)
    pltpu.make_async_copy(cache, cache, cache_send.at[0]).wait()
    pltpu.make_async_copy(cache, cache, cache_send.at[1]).wait()
    pltpu.make_async_copy(cache, cache, cache_recv.at[0]).wait()


def attend_kernel(
    slot_ref,
    len_ref,
    arr,
    proj,
    cos_ref,
    sin_ref,
    kv,
    served,
    context,
    queries,
    scores,
    probs,
    outs,
    served_sem,
):
    def install(b):
        pltpu.make_async_copy(
            arr.at[slot_ref[b]], served.at[0, pl.ds(pl.multiple_of(b * BROWS, BROWS), BROWS)], served_sem.at[0]
        ).start()

    def install_all(b, carry):
        install(b)
        return carry

    lax.fori_loop(0, NB, install_all, 0, unroll=8)

    def rotate(block):
        return (block * cos_ref[...] + pltpu.roll(block, HD // 2, 1) * sin_ref[...]).astype(jnp.bfloat16)

    for head in range(HEADS):
        turned = rotate(proj[:, pl.ds(head * HD, HD)]).astype(jnp.float32)
        for s in range(STEPS):
            queries[:, s * HEADS + head, :] = turned[s * ROWS : (s + 1) * ROWS]
    keys_new = rotate(proj[:, pl.ds(QC, HD)]).astype(jnp.float32).reshape(STEPS, ROWS, 1, HD)
    values_new = proj[:, pl.ds(QC + HD, HD)].astype(jnp.bfloat16).astype(jnp.float32)
    values_new = values_new.reshape(STEPS, ROWS, 1, HD)

    scale_factor = HD ** (-0.5)
    position = lax.broadcasted_iota(jnp.int32, (1, LEN), 1)
    dims = (((1,), (1,)), ((), ()))

    def score(b, carry):
        found = lax.dot_general(
            queries[b].astype(jnp.bfloat16), kv[b, :, :HD], dims, preferred_element_type=jnp.float32
        )
        scores[b] = jnp.where(position < len_ref[b], found * scale_factor, masked_score)
        return carry

    lax.fori_loop(0, ROWS, score, 0, unroll=8)

    query = queries[...]
    fresh = [jnp.sum(query * keys_new[s], axis=-1, keepdims=True) * scale_factor for s in range(STEPS)]
    step = lax.broadcasted_iota(jnp.int32, (ROWS, STEPS * HEADS, 1), 1) // HEADS
    fresh[1] = jnp.where(step >= 1, fresh[1], masked_score)
    found = scores[...]
    peaks = jnp.maximum(jnp.max(found, axis=-1, keepdims=True), jnp.maximum(fresh[0], fresh[1]))
    weights = jnp.exp(found - peaks).astype(jnp.bfloat16)
    probs[...] = weights
    total = jnp.sum(weights.astype(jnp.float32), axis=-1, keepdims=True)
    fresh = [jnp.exp(one - peaks).astype(jnp.bfloat16).astype(jnp.float32) for one in fresh]
    total = total + fresh[0] + fresh[1]
    extra = fresh[0] * values_new[0] + fresh[1] * values_new[1]

    def gather(b, carry):
        outs[b] = jnp.dot(probs[b], kv[b, :, HD:], preferred_element_type=jnp.float32)
        return carry

    lax.fori_loop(0, ROWS, gather, 0, unroll=16)
    outs[...] = (outs[...] + extra) / total
    for head in range(HEADS):
        for s in range(STEPS):
            context[pl.ds(s * ROWS, ROWS), pl.ds(head * HD, HD)] = outs[:, s * HEADS + head, :].astype(jnp.bfloat16)
    pltpu.make_async_copy(served, served, served_sem.at[0]).wait()


def on_device(hidden_in, norm_gain, qkv_buckets, bucket_slot, kv_cache, cache_len):
    any_space = pl.BlockSpec(memory_space=pl.ANY)
    vmem = pl.BlockSpec(memory_space=pltpu.VMEM)
    smem = pl.BlockSpec(memory_space=pltpu.SMEM)
    freqs = rope_base ** (-2.0 * jnp.arange(HD // 2, dtype=jnp.float32) / HD)
    freqs = jnp.concatenate([freqs, freqs]).reshape(1, HD)
    dma = pltpu.SemaphoreType.DMA
    in_hbm = functools.partial(pltpu.with_memory_space_constraint, memory_space=pltpu.HBM)
    in_vmem = functools.partial(pltpu.with_memory_space_constraint, memory_space=pltpu.VMEM)
    arr, proj, cosine, sine, kv = pl.pallas_call(
        gather_kernel,
        out_shape=[
            pltpu.VMEM((NB, BROWS, COLS), jnp.bfloat16),
            pltpu.VMEM((M, COLS), jnp.float32),
            pltpu.VMEM((M, HD), jnp.float32),
            pltpu.VMEM((M, HD), jnp.float32),
            pltpu.VMEM((ROWS, LEN, 2 * HD), jnp.bfloat16),
        ],
        in_specs=[any_space] * 5 + [vmem, any_space],
        out_specs=[vmem] * 5,
        scratch_shapes=[
            pltpu.VMEM((M, D), jnp.bfloat16),
            pltpu.VMEM((1, D), jnp.float32),
            pltpu.VMEM((1, NB), jnp.int32),
            pltpu.VMEM((1, NB), jnp.int32),
            pltpu.SMEM((1, NB), jnp.int32),
            pltpu.SMEM((ROWS,), jnp.int32),
            pltpu.VMEM((M, HD), jnp.float32),
            pltpu.VMEM((NB, BROWS, M), jnp.bfloat16),
            pltpu.VMEM((NB // 4, M, 4 * BROWS), jnp.bfloat16),
            dma((5,)),
            dma((2,)),
            dma((len(SHARED),)),
            dma((1,)),
            dma((len(DIRECT),)),
            dma((len(UNITS),)),
            dma((3,)),
            dma((1,)),
            dma((1,)),
            dma((len(GROUP_ENDS),)),
            dma((2,)),
            dma((1,)),
        ],
        compiler_params=pltpu.CompilerParams(
            collective_id=0, has_side_effects=True, vmem_limit_bytes=10 * 2**20
        ),
        name="gather_and_project",
    )(
        in_hbm(hidden_in.reshape(M, D)),
        in_hbm(norm_gain.reshape(1, D)),
        in_hbm(qkv_buckets),
        in_hbm(bucket_slot.reshape(1, NB)),
        in_hbm(kv_cache),
        freqs,
        in_hbm(cache_len),
    )
    served, context = pl.pallas_call(
        attend_kernel,
        out_shape=[
            pltpu.HBM((1, D, COLS), jnp.bfloat16),
            jax.ShapeDtypeStruct((M, QC), jnp.bfloat16),
        ],
        in_specs=[smem, smem] + [vmem] * 5,
        out_specs=[any_space, vmem],
        scratch_shapes=[
            pltpu.VMEM((ROWS, STEPS * HEADS, HD), jnp.float32),
            pltpu.VMEM((ROWS, STEPS * HEADS, LEN), jnp.float32),
            pltpu.VMEM((ROWS, STEPS * HEADS, LEN), jnp.bfloat16),
            pltpu.VMEM((ROWS, STEPS * HEADS, HD), jnp.float32),
            dma((1,)),
        ],
        compiler_params=pltpu.CompilerParams(vmem_limit_bytes=12 * 2**20),
        name="attend_and_install",
    )(in_hbm(bucket_slot), in_hbm(cache_len), in_vmem(arr), in_vmem(proj), in_vmem(cosine), in_vmem(sine), in_vmem(kv))
    return context.reshape(STEPS, ROWS, QC), served


def solution(mesh):
    in_specs = (
        P(None, "replica", None),
        P(),
        P(("replica", "tensor"), None, None),
        P(),
        P("replica", "tensor", None),
        P("replica"),
    )
    out_specs = (P(None, "replica", "tensor"), P("tensor", None, None))
    return jax.shard_map(
        on_device, mesh=mesh, in_specs=in_specs, out_specs=out_specs, check_vma=False
    )
```

```python
import functools
import heapq
import itertools

import jax
import jax.numpy as jnp
import numpy as np
from jax import lax
from jax.experimental import pallas as pl
from jax.experimental.pallas import tpu as pltpu
from jax.sharding import PartitionSpec as P

QH = 64
KVH = 8
HD = 128
D = 8192
LEN = 2048
STEPS = 2
BROWS = 32
NB = 256
N_TENSOR = 16
N_REPLICA = 8
ROWS = 16
M = STEPS * ROWS
QC = 512
OWN = QC + HD
COLS = QC + 2 * HD
HEADS = QC // HD
HALF = LEN // 2

rope_base = 500000.0
norm_eps = 1e-05
masked_score = -1e30

MESH = pl.DeviceIdType.MESH

UNITS = ((0, 0), (1, 0), (3, 0), (0, 1), (1, 1), (3, 1), (2, 0), (2, 1))
ITEMS = ((0, 0, 2), (0, 2, 2)) + tuple((u, 0, 4) for u in range(1, 8))
PAIR_FIRST = frozenset((0, 2, 3, 7, 8))


def event_order():
    per_slot, hop = 0.87, 2.5
    entry = (0.7, 0.7, 5.0, 5.0, 5.5, 10.0, 11.0, 15.0, 18.0)
    links = ("pair", "up", "down")
    free = dict.fromkeys(links, 0.0)
    queue = {link: [] for link in links}
    count = itertools.count()
    events = [(entry[i], next(count), ("entry", i)) for i in range(len(ITEMS))]
    heapq.heapify(events)
    order = []
    while events:
        now, _, event = heapq.heappop(events)
        if event is not None:
            order.append(event)
            for link, arrival, slots in forwards(event):
                queue[link].append((arrival, slots))
        for link in links:
            if queue[link] and free[link] <= now + 1e-9:
                arrival, slots = queue[link].pop(0)
                free[link] = now + slots * per_slot
                heapq.heappush(events, (free[link] + hop, next(count), arrival))
                heapq.heappush(events, (free[link], next(count), None))
    return order


def forwards(event):
    kind, item = event[0], event[1]
    slots = ITEMS[item][2]
    sends = []
    if kind == "entry":
        sends += [("pair", ("pair", item), slots)]
        sends += [("up", ("up1", item, 0), slots), ("down", ("down1", item, 0), slots)]
    elif kind == "pair" and item in PAIR_FIRST:
        sends += [("up", ("up1", item, 1), slots), ("down", ("down1", item, 1), slots)]
    elif kind in ("up1", "down1"):
        link = kind[:-1]
        sends += [(link, (link + "2", item, event[2]), slots // 2)]
        if item not in PAIR_FIRST:
            sends += [("pair", ("late", item, kind), slots)]
    elif kind in ("up2", "down2") and item not in PAIR_FIRST:
        sends += [("pair", ("late", item, kind), slots // 2)]
    return sends


EVENTS = event_order()
PLACE = {event: i for i, event in enumerate(EVENTS)}
ARRIVALS = [event for event in EVENTS if event[0] != "entry"]
BOTH = {"up1": "round1", "down1": "round1", "up2": "round2", "down2": "round2"}
SHARED = list(dict.fromkeys((BOTH.get(event[0], event[0]),) + event[1:] for event in ARRIVALS))
RECV = {event: SHARED.index((BOTH.get(event[0], event[0]),) + event[1:]) for event in ARRIVALS}
DIRECT = {event: i for i, event in enumerate(EVENTS[-3:])}
GROUP_ENDS = (14, 28, 42, 56, 68, 78, 82, 85, len(EVENTS) - len(DIRECT))
GROUP = {event: sum(PLACE[event] >= end for end in GROUP_ENDS) for event in EVENTS}


def gather_kernel(
    hid_hbm,
    gain_hbm,
    buckets,
    slot_hbm,
    cache,
    freq_ref,
    len_hbm,
    arr,
    proj,
    cos_ref,
    sin_ref,
    kv,
    slot_row,
    len_row,
    hid,
    gain,
    inv_row,
    inv,
    len_ref,
    factor,
    turned,
    lhs,
    prep_sem,
    own_sem,
    recv_sem,
    direct_send,
    direct_recv,
    entry_sem,
    link_sem,
    stage_sem,
    kv_send,
    kv_recv,
    cache_send,
    cache_recv,
):
    r = lax.axis_index("replica")
    t = lax.axis_index("tensor")
    z, p = r // 2, r % 2
    x, h, c = t // 4, (t // 2) % 2, t % 2
    other_core = (r, x * 4 + h * 2 + (1 - c))
    next_replica = {
        "pair": z * 2 + (1 - p),
        "up": ((z + 1) % 4) * 2 + p,
        "down": ((z + 3) % 4) * 2 + p,
    }
    target = {link: (replica, t) for link, replica in next_replica.items()}
    across = {link: (replica, other_core[1]) for link, replica in next_replica.items()}
    own_col = pl.multiple_of(QC + HD * c, HD)
    other_col = pl.multiple_of(QC + HD * (1 - c), HD)

    prep = [
        pltpu.make_async_copy(hid_hbm, hid, prep_sem.at[0]),
        pltpu.make_async_copy(gain_hbm, gain, prep_sem.at[1]),
        pltpu.make_async_copy(slot_hbm, slot_row, prep_sem.at[2]),
        pltpu.make_async_copy(len_hbm, len_ref, prep_sem.at[3]),
        pltpu.make_async_copy(len_hbm, len_row, prep_sem.at[5]),
    ]
    for copy in prep:
        copy.start()

    def chip(dx, dh, core):
        return (z * 2 + (p + dh) % 2, ((x + dx) % 4) * 4 + ((h + dh) % 2) * 2 + core)

    barrier = pltpu.get_barrier_semaphore()
    peers = [other_core] + list(target.values()) + list(across.values())
    peers += [chip(dx, dh, core) for dx, dh in UNITS[1:4] for core in range(2)]
    for peer in peers:
        pl.semaphore_signal(barrier, inc=1, device_id=peer, device_id_type=MESH)
    pl.semaphore_wait(barrier, len(peers))

    mine = (r * N_TENSOR + t) * 2
    sent = {"pair": 0, "up": 0, "down": 0}
    link_index = {"pair": 0, "up": 1, "down": 2}

    def parts(base, slots):
        rows = pl.ds(base, slots)
        return arr.at[rows, :, pl.ds(own_col, HD)], arr.at[rows, :, pl.ds(0, QC)]

    def bucket_parts(x_to, h_to, core):
        group = x_to * 2 + h_to
        query = pl.multiple_of((group * 2 + core) * QC, QC)
        key = pl.multiple_of(QH * HD + core * (KVH * HD) + group * HD, HD)
        return buckets.at[:, :, pl.ds(key, HD)], buckets.at[:, :, pl.ds(query, QC)]

    def own_columns(core):
        return pl.ds(pl.multiple_of(QC + HD * core, HD), HD), pl.ds(0, QC)

    def send_mine(x_to, h_to, core, dst, send_sem, recv_sems):
        for src, cols, recv in zip(bucket_parts(x_to, h_to, core), own_columns(core), recv_sems):
            pltpu.make_async_remote_copy(
                src_ref=src,
                dst_ref=arr.at[pl.ds(mine, 2), :, cols],
                send_sem=send_sem,
                recv_sem=recv,
                device_id=dst,
                device_id_type=MESH,
            ).start()

    def send_unit(unit):
        dx, dh = UNITS[unit]
        x_to, h_to, p_to = (x + 4 - dx) % 4, (h + dh) % 2, (p + dh) % 2
        sems = (entry_sem.at[unit], entry_sem.at[unit])
        for core in range(2):
            dst = (z * 2 + p_to, x_to * 4 + h_to * 2 + core)
            send_mine(x_to, h_to, core, dst, stage_sem.at[0], sems)

    def wait_bytes(slots, sem, width=OWN):
        ref = arr.at[pl.ds(0, slots), :, pl.ds(0, width)]
        pltpu.make_async_copy(ref, ref, sem).wait()

    def recv_of(event):
        return recv_sem.at[RECV[event]]

    for item, core in ((0, c), (1, 1 - c)):
        for link, arrival, slots in forwards(("entry", item)):
            dst = (target, across)[item][link]
            sems = (recv_of(arrival), recv_of(arrival))
            send_mine(x, h, core, dst, link_sem.at[link_index[link]], sems)
            sent[link] += slots
    own_copies = []
    for src, dst in zip(bucket_parts(x, h, c), parts(mine, 2)):
        copy = pltpu.make_async_copy(src, dst, own_sem.at[len(own_copies)])
        copy.start()
        own_copies.append(copy)
    send_mine(x, h, 1 - c, other_core, stage_sem.at[0], (entry_sem.at[0], entry_sem.at[0]))
    for unit in (1, 2, 3):
        send_unit(unit)

    def unit_base(unit, z_of, p_of):
        dx, dh = UNITS[unit]
        source = z_of * 2 + (p_of + dh) % 2
        return source * 32 + ((x + dx) % 4) * 8 + ((h + dh) % 2) * 4

    up_z, down_z, far_z = (z + 3) % 4, (z + 1) % 4, (z + 2) % 4

    def place(event):
        kind, item = event[0], event[1]
        unit, first, slots = ITEMS[item]
        if kind == "entry":
            z_of, p_of = z, p
        elif kind == "pair":
            z_of, p_of = z, 1 - p
        else:
            way = event[2] if kind == "late" else kind
            z_of = {"up1": up_z, "down1": down_z, "up2": far_z, "down2": far_z}[way]
            if kind == "late":
                p_of = 1 - p
            else:
                p_of = (p + event[2]) % 2
            if way in ("up2", "down2"):
                slots = slots // 2
                if way == "down2":
                    first = first + slots
        base = unit_base(unit, z_of, p_of)
        if unit == 0:
            own_half = 2 * c if item == 0 else 2 * (1 - c)
            base = base + own_half + (first - ITEMS[item][1])
        else:
            base = base + first
        return base, slots

    waited = set()

    def wait_for(event):
        slots = place(event)[1]
        if event == ("entry", 0):
            for copy in own_copies:
                copy.wait()
        elif event == ("entry", 1):
            wait_bytes(slots, entry_sem.at[0])
        elif event[0] == "entry":
            wait_bytes(slots, entry_sem.at[ITEMS[event[1]][0]])
        elif event[0] not in BOTH:
            wait_bytes(slots, recv_of(event))
        elif RECV[event] not in waited:
            waited.add(RECV[event])
            wait_bytes(2 * slots, recv_of(event))

    def forward(event):
        if event in (("entry", 0), ("entry", 1)):
            return
        base, _ = place(event)
        for link, arrival, slots in forwards(event):
            start = base
            if arrival[0] == "down2":
                start = base + slots
            sends = [(ref, target[link], link_sem.at[link_index[link]], recv_of(arrival)) for ref in parts(start, slots)]
            if arrival in DIRECT:
                sends.insert(0, (sends[0][0], across[link], direct_send.at[0], direct_recv.at[DIRECT[arrival]]))
            for ref, dst, send_sem, recv in sends:
                pltpu.make_async_remote_copy(
                    src_ref=ref,
                    dst_ref=ref,
                    send_sem=send_sem,
                    recv_sem=recv,
                    device_id=dst,
                    device_id_type=MESH,
                ).start()
            sent[link] += slots

    def share(event):
        base, slots = place(event)
        ref = arr.at[pl.ds(base, slots), :, pl.ds(own_col, HD)]
        pltpu.make_async_remote_copy(
            src_ref=ref,
            dst_ref=ref,
            send_sem=kv_send.at[0],
            recv_sem=kv_recv.at[GROUP[event]],
            device_id=other_core,
            device_id_type=MESH,
        ).start()

    group_slots = [0] * len(GROUP_ENDS)
    for event in EVENTS:
        if event not in DIRECT:
            group_slots[GROUP[event]] += place(event)[1]
    direct_slots = [place(event)[1] for event in DIRECT]

    def shared_wait(group):
        ref = arr.at[pl.ds(0, group_slots[group]), :, pl.ds(QC, HD)]
        pltpu.make_async_copy(ref, ref, kv_recv.at[group]).wait()

    own_half = pl.ds(pl.multiple_of(c * HALF, HALF), HALF)

    def send_cache(row):
        pltpu.make_async_copy(cache.at[row], kv.at[row, own_half], cache_send.at[1]).start()
        pltpu.make_async_remote_copy(
            src_ref=cache.at[row],
            dst_ref=kv.at[row, own_half],
            send_sem=cache_send.at[0],
            recv_sem=cache_recv.at[0],
            device_id=other_core,
            device_id_type=MESH,
        ).start()

    def squares(j, total):
        part = hid[:, pl.ds(pl.multiple_of(j * 512, 512), 512)].astype(jnp.float32)
        return total + jnp.sum(part * part, axis=-1, keepdims=True)

    def turn(j, carry):
        cols = pl.ds(pl.multiple_of(j * 128, 128), 128)
        part = hid[:, cols].astype(jnp.float32) * factor[...] * gain[:, cols]
        part = part.astype(jnp.bfloat16).astype(jnp.float32)
        part = jnp.transpose(part).astype(jnp.bfloat16)
        turned[pl.ds(j * 4, 4)] = part.reshape(4, BROWS, M)
        return carry

    def pick(j, carry):
        rows = [turned[inv[0, j * 4 + i]] for i in range(4)]
        part = jnp.concatenate(rows, axis=0).astype(jnp.float32)
        lhs[j] = jnp.transpose(part).astype(jnp.bfloat16)
        return carry

    move = pltpu.make_async_copy(inv_row, inv, prep_sem.at[4])

    def find_slots():
        for copy in prep:
            copy.wait()
        slots = jnp.broadcast_to(slot_row[...], (NB, NB))
        by_bucket = jnp.transpose(slots)
        hit = by_bucket == lax.broadcasted_iota(jnp.int32, (NB, NB), 1)
        bucket = lax.broadcasted_iota(jnp.int32, (NB, NB), 0)
        inv_row[...] = jnp.max(jnp.where(hit, bucket, 0), axis=0, keepdims=True)
        move.start()

    def find_factor():
        total = lax.fori_loop(0, D // 512, squares, jnp.zeros((M, 1), jnp.float32))
        factor[...] = jnp.broadcast_to(lax.rsqrt(total * (1.0 / D) + norm_eps), (M, HD))
        move.wait()

    def find_angles():
        row = lax.broadcasted_iota(jnp.int32, (M, HD), 0)
        position = jnp.zeros((M, HD), jnp.int32)
        for b in range(ROWS):
            for s in range(STEPS):
                position = jnp.where(row == s * ROWS + b, len_ref[0, b] + s, position)
        angle = position.astype(jnp.float32) * freq_ref[...]
        lane = lax.broadcasted_iota(jnp.int32, (M, HD), 1)
        cos_ref[...] = jnp.cos(angle)
        sine = jnp.sin(angle)
        sin_ref[...] = jnp.where(lane < HD // 2, -sine, sine)
        proj[...] = jnp.zeros_like(proj)

    slices = 8
    span = D // 128 // slices
    prepare = [find_slots, find_factor, find_angles]
    for body in (turn, pick):
        for i in range(slices):
            prepare.append(functools.partial(lax.fori_loop, i * span, (i + 1) * span, body, 0))
    prepare = iter(prepare)

    def multiply(base, column, width):
        rows = arr[pl.ds(base, 4), :, pl.ds(column, width)].reshape(4 * BROWS, width)
        return jnp.dot(lhs[base // 4], rows, preferred_element_type=jnp.float32)

    def add_own(base):
        base = pl.multiple_of(base, 4)
        proj[:, :QC] += multiply(base, 0, QC)
        proj[:, pl.ds(own_col, HD)] += multiply(base, own_col, HD)

    def add_other(base):
        base = pl.multiple_of(base, 4)
        proj[:, pl.ds(other_col, HD)] += multiply(base, other_col, HD)

    def unit_of(event):
        kind, item = event[0], event[1]
        unit = ITEMS[item][0]
        if kind in ("entry", "pair"):
            return (kind, unit)
        way = event[2] if kind == "late" else kind
        side = 1 if kind == "late" else event[2]
        far = way in ("up2", "down2")
        return ("far" if far else way, side, unit)

    missing = {}
    for event in EVENTS:
        missing.setdefault(unit_of(event), set()).add(event)
    base_of = {}
    ready = []
    for name, members in missing.items():
        some = next(event for event in EVENTS if event in members)
        kind = some[0]
        if kind == "entry":
            base_of[name] = unit_base(name[1], z, p)
        elif kind == "pair":
            base_of[name] = unit_base(name[1], z, 1 - p)
        else:
            z_of = {"up1": up_z, "down1": down_z, "far": far_z}[name[0]]
            base_of[name] = unit_base(name[2], z_of, (p + name[1]) % 2)
    members_of = {name: sorted(events, key=PLACE.get) for name, events in missing.items()}
    waiting_other = []
    shared = set()
    prepared = False
    cache_rows = iter(range(ROWS))
    for step, event in enumerate(EVENTS):
        wait_for(event)
        forward(event)
        if event not in DIRECT:
            share(event)
        if event == ("entry", 4):
            for unit in (4, 5, 6):
                send_unit(unit)
        if event == ("entry", 5):
            send_unit(7)
        name = unit_of(event)
        missing[name].remove(event)
        if not missing[name]:
            ready.append(name)
        if step >= 20 and not prepared:
            work = next(prepare, None)
            if work is None:
                prepared = True
            else:
                work()
        if step >= 12:
            row = next(cache_rows, None)
            if row is not None:
                send_cache(row)
        if prepared:
            for name in ready[:2]:
                add_own(base_of[name])
                waiting_other.append(name)
            ready = ready[2:]
            for name in waiting_other[:2]:
                group = max(GROUP[member] for member in members_of[name])
                if group < len(GROUP_ENDS) and step >= GROUP_ENDS[group] + 2:
                    for earlier in range(group + 1):
                        if earlier not in shared:
                            shared_wait(earlier)
                            shared.add(earlier)
                    add_other(base_of[name])
                    waiting_other.remove(name)
    for name in ready:
        add_own(base_of[name])
        waiting_other.append(name)
    for group in range(len(GROUP_ENDS)):
        if group not in shared:
            shared_wait(group)
    for i, slots in enumerate(direct_slots):
        wait_bytes(slots, direct_recv.at[i], HD)
    for name in waiting_other:
        add_other(base_of[name])

    for link, slots in sent.items():
        wait_bytes(slots, link_sem.at[link_index[link]])
    wait_bytes(30, stage_sem.at[0])
    wait_bytes(sum(group_slots), kv_send.at[0], HD)
    wait_bytes(sum(direct_slots), direct_send.at[0], HD)
    pltpu.make_async_copy(cache, cache, cache_send.at[0]).wait()
    pltpu.make_async_copy(cache, cache, cache_send.at[1]).wait()
    pltpu.make_async_copy(cache, cache, cache_recv.at[0]).wait()


def attend_kernel(
    slot_row,
    len_row,
    arr,
    proj,
    cos_ref,
    sin_ref,
    kv,
    served,
    context,
    queries,
    scores,
    probs,
    outs,
    slot_ref,
    len_ref,
    row_sem,
    served_sem,
):
    rows = [
        pltpu.make_async_copy(slot_row, slot_ref, row_sem.at[0]),
        pltpu.make_async_copy(len_row, len_ref, row_sem.at[1]),
    ]
    for copy in rows:
        copy.start()
    for copy in rows:
        copy.wait()

    def install(b):
        pltpu.make_async_copy(
            arr.at[slot_ref[0, b]], served.at[0, pl.ds(pl.multiple_of(b * BROWS, BROWS), BROWS)], served_sem.at[0]
        ).start()

    def install_all(b, carry):
        install(b)
        return carry

    lax.fori_loop(0, NB, install_all, 0, unroll=8)

    def rotate(block):
        return (block * cos_ref[...] + pltpu.roll(block, HD // 2, 1) * sin_ref[...]).astype(jnp.bfloat16)

    for head in range(HEADS):
        turned = rotate(proj[:, pl.ds(head * HD, HD)]).astype(jnp.float32)
        for s in range(STEPS):
            queries[:, s * HEADS + head, :] = turned[s * ROWS : (s + 1) * ROWS]
    keys_new = rotate(proj[:, pl.ds(QC, HD)]).astype(jnp.float32).reshape(STEPS, ROWS, 1, HD)
    values_new = proj[:, pl.ds(QC + HD, HD)].astype(jnp.bfloat16).astype(jnp.float32)
    values_new = values_new.reshape(STEPS, ROWS, 1, HD)

    scale_factor = HD ** (-0.5)
    position = lax.broadcasted_iota(jnp.int32, (1, LEN), 1)
    dims = (((1,), (1,)), ((), ()))

    def score(b, carry):
        found = lax.dot_general(
            queries[b].astype(jnp.bfloat16), kv[b, :, :HD], dims, preferred_element_type=jnp.float32
        )
        scores[b] = jnp.where(position < len_ref[0, b], found * scale_factor, masked_score)
        return carry

    lax.fori_loop(0, ROWS, score, 0, unroll=8)

    query = queries[...]
    fresh = [jnp.sum(query * keys_new[s], axis=-1, keepdims=True) * scale_factor for s in range(STEPS)]
    step = lax.broadcasted_iota(jnp.int32, (ROWS, STEPS * HEADS, 1), 1) // HEADS
    fresh[1] = jnp.where(step >= 1, fresh[1], masked_score)
    found = scores[...]
    peaks = jnp.maximum(jnp.max(found, axis=-1, keepdims=True), jnp.maximum(fresh[0], fresh[1]))
    weights = jnp.exp(found - peaks).astype(jnp.bfloat16)
    probs[...] = weights
    total = jnp.sum(weights.astype(jnp.float32), axis=-1, keepdims=True)
    fresh = [jnp.exp(one - peaks).astype(jnp.bfloat16).astype(jnp.float32) for one in fresh]
    total = total + fresh[0] + fresh[1]
    extra = fresh[0] * values_new[0] + fresh[1] * values_new[1]

    def gather(b, carry):
        outs[b] = jnp.dot(probs[b], kv[b, :, HD:], preferred_element_type=jnp.float32)
        return carry

    lax.fori_loop(0, ROWS, gather, 0, unroll=16)
    outs[...] = (outs[...] + extra) / total
    for head in range(HEADS):
        for s in range(STEPS):
            context[pl.ds(s * ROWS, ROWS), pl.ds(head * HD, HD)] = outs[:, s * HEADS + head, :].astype(jnp.bfloat16)
    pltpu.make_async_copy(served, served, served_sem.at[0]).wait()


def on_device(hidden_in, norm_gain, qkv_buckets, bucket_slot, kv_cache, cache_len):
    any_space = pl.BlockSpec(memory_space=pl.ANY)
    vmem = pl.BlockSpec(memory_space=pltpu.VMEM)
    smem = pl.BlockSpec(memory_space=pltpu.SMEM)
    freqs = rope_base ** (-2.0 * jnp.arange(HD // 2, dtype=jnp.float32) / HD)
    freqs = jnp.concatenate([freqs, freqs]).reshape(1, HD)
    dma = pltpu.SemaphoreType.DMA
    in_hbm = functools.partial(pltpu.with_memory_space_constraint, memory_space=pltpu.HBM)
    in_vmem = functools.partial(pltpu.with_memory_space_constraint, memory_space=pltpu.VMEM)
    arr, proj, cosine, sine, kv, slots, lengths = pl.pallas_call(
        gather_kernel,
        out_shape=[
            pltpu.VMEM((NB, BROWS, COLS), jnp.bfloat16),
            pltpu.VMEM((M, COLS), jnp.float32),
            pltpu.VMEM((M, HD), jnp.float32),
            pltpu.VMEM((M, HD), jnp.float32),
            pltpu.VMEM((ROWS, LEN, 2 * HD), jnp.bfloat16),
            pltpu.VMEM((1, NB), jnp.int32),
            pltpu.VMEM((1, ROWS), jnp.int32),
        ],
        in_specs=[any_space] * 5 + [vmem, any_space],
        out_specs=[vmem] * 7,
        scratch_shapes=[
            pltpu.VMEM((M, D), jnp.bfloat16),
            pltpu.VMEM((1, D), jnp.float32),
            pltpu.VMEM((1, NB), jnp.int32),
            pltpu.SMEM((1, NB), jnp.int32),
            pltpu.SMEM((1, ROWS), jnp.int32),
            pltpu.VMEM((M, HD), jnp.float32),
            pltpu.VMEM((NB, BROWS, M), jnp.bfloat16),
            pltpu.VMEM((NB // 4, M, 4 * BROWS), jnp.bfloat16),
            dma((6,)),
            dma((2,)),
            dma((len(SHARED),)),
            dma((1,)),
            dma((len(DIRECT),)),
            dma((len(UNITS),)),
            dma((3,)),
            dma((1,)),
            dma((1,)),
            dma((len(GROUP_ENDS),)),
            dma((2,)),
            dma((1,)),
        ],
        compiler_params=pltpu.CompilerParams(
            collective_id=0, has_side_effects=True, vmem_limit_bytes=10 * 2**20
        ),
        name="gather_and_project",
    )(
        in_hbm(hidden_in.reshape(M, D)),
        in_hbm(norm_gain.reshape(1, D)),
        in_hbm(qkv_buckets),
        in_hbm(bucket_slot.reshape(1, NB)),
        in_hbm(kv_cache),
        freqs,
        in_hbm(cache_len.reshape(1, ROWS)),
    )
    served, context = pl.pallas_call(
        attend_kernel,
        out_shape=[
            pltpu.HBM((1, D, COLS), jnp.bfloat16),
            jax.ShapeDtypeStruct((M, QC), jnp.bfloat16),
        ],
        in_specs=[vmem] * 7,
        out_specs=[any_space, vmem],
        scratch_shapes=[
            pltpu.VMEM((ROWS, STEPS * HEADS, HD), jnp.float32),
            pltpu.VMEM((ROWS, STEPS * HEADS, LEN), jnp.float32),
            pltpu.VMEM((ROWS, STEPS * HEADS, LEN), jnp.bfloat16),
            pltpu.VMEM((ROWS, STEPS * HEADS, HD), jnp.float32),
            pltpu.SMEM((1, NB), jnp.int32),
            pltpu.SMEM((1, ROWS), jnp.int32),
            dma((2,)),
            dma((1,)),
        ],
        compiler_params=pltpu.CompilerParams(vmem_limit_bytes=12 * 2**20),
        name="attend_and_install",
    )(in_vmem(slots), in_vmem(lengths), in_vmem(arr), in_vmem(proj), in_vmem(cosine), in_vmem(sine), in_vmem(kv))
    return context.reshape(STEPS, ROWS, QC), served


def solution(mesh):
    in_specs = (
        P(None, "replica", None),
        P(),
        P(("replica", "tensor"), None, None),
        P(),
        P("replica", "tensor", None),
        P("replica"),
    )
    out_specs = (P(None, "replica", "tensor"), P("tensor", None, None))
    return jax.shard_map(
        on_device, mesh=mesh, in_specs=in_specs, out_specs=out_specs, check_vma=False
    )
```
